1024 devices in a mesh: seq: 64 (over z, x), mp: 16 (over y, core).
Axes of the slice: x: 4, y: 8, z: 16, core: 2. Of those that a mesh axis runs over, the one named last changes fastest.
Arguments:
- hidden_state: bfloat16 [32768, 4096], P('seq', 'mp'), may hold values from -16 to 16
- router_weight: float32 [32768], P('seq'), may hold values from 0.2 to 1
- norm_gain: float32 [4096], replicated, may hold values from 0.5 to 1.5
- query_weight: bfloat16 [4096, 4096], P(None, 'mp'), may hold values from -1 to 1
- kv_weight: bfloat16 [4096, 2048], P(None, 'mp'), may hold values from -1 to 1
- out_weight: bfloat16 [4096, 4096], P('mp'), may hold values from -0.09375 to 0.09375
- sel_rows: int32 [8192], P('seq'), may hold values from -1 to 511, as said below
- dest_shard: int32 [8192], P('seq'), may hold values from -1 to 63, as said below
- dest_slot: int32 [8192], P('seq'), may hold values from -1 to 63, as said below
Outputs:
- mixed: bfloat16 [32768, 4096], P('seq', 'mp')
The draws below stay inside these ranges and needn't reach their ends.
Inputs may be any that keep to these rules, and one draw needn't show every extreme that they name: `sel_rows`: within a shard the used entries come first, -1 after them; used rows are distinct and ascending. `dest_shard`: A shard's used entries take consecutive ranks in order, shards in order; the token of rank q goes to shard q mod 64; -1 on unused entries. Some shard uses all 128 entries, so 2 tokens go from it to one shard, and every shard receives exactly 64. `dest_slot`: the slot of the token of rank q is q // 64; -1 on unused entries.
All inputs are finite; a program needn't handle non-finite values.
Results may differ from the reference program's by a relative error of at most 0.0045.
Values may be sent and summed in bfloat16 or wider, within the bound.
No kernel may reach another device: no remote copies, remote signals or barrier semaphores. Data moves between devices by JAX's collectives and lax.ppermute only.
A program may use at most 32 MiB of HBM per device.

```python
import math
import jax
import jax.numpy as jnp
from jax import lax

D = 4096
HEADS = 32
KV_HEADS = 8
HEAD_DIM = 128
TOK_DEV = 512
SEL_DEV = 64
SEL_CAP = 128
TOKENS = 32768
SELECTED = 4096
N_SEQ = 64
N_MP = 16


def chosen_tokens(key):
    shard_count = TOKENS // TOK_DEV
    half_count = shard_count // 2
    order = jax.random.permutation(jax.random.fold_in(key, 11), shard_count)
    spread = jax.random.randint(jax.random.fold_in(key, 12), (half_count,), 0, SEL_DEV + 1)
    spread = spread.at[0].set(SEL_DEV)
    counts = jnp.zeros((shard_count,), jnp.int32)
    counts = counts.at[order[:half_count]].set(SEL_DEV + spread)
    counts = counts.at[order[half_count:]].set(SEL_DEV - spread)
    offsets = jnp.cumsum(counts) - counts
    shard_keys = jax.random.split(jax.random.fold_in(key, 13), shard_count)
    shuffled = jax.vmap(lambda item: jax.random.permutation(item, TOK_DEV))(shard_keys)
    columns = jnp.arange(TOK_DEV, dtype=jnp.int32)[None, :]
    picked = shuffled < counts[:, None]
    ordered = jnp.sort(jnp.where(picked, columns, TOK_DEV + columns), axis=1)[:, :SEL_CAP]
    places = jnp.arange(SEL_CAP, dtype=jnp.int32)[None, :]
    usable = places < counts[:, None]
    rank_order = offsets[:, None] + places
    rows_out = jnp.where(usable, ordered, -1)
    shards_out = jnp.where(usable, rank_order % shard_count, -1)
    slots_out = jnp.where(usable, rank_order // shard_count, -1)
    return (rows_out.reshape(-1), shards_out.reshape(-1), slots_out.reshape(-1))


def draw_sel_rows(key, part):
    rows_out, shards_out, slots_out = chosen_tokens(key)
    return rows_out


def draw_dest_shard(key, part):
    rows_out, shards_out, slots_out = chosen_tokens(key)
    return shards_out


def draw_dest_slot(key, part):
    rows_out, shards_out, slots_out = chosen_tokens(key)
    return slots_out


def draw_hidden_state(key, part):
    key = jax.random.fold_in(key, 1)
    base = jnp.clip(jax.random.normal(key, (TOKENS, D), jnp.float32), -6.0, 6.0)
    return base.astype(jnp.bfloat16)


def draw_query_weight(key, part):
    key = jax.random.fold_in(key, 2)
    matrix = jnp.clip(jax.random.normal(key, (D, HEADS * HEAD_DIM), jnp.float32), -6.0, 6.0) * math.sqrt(3.0 / D)
    return matrix.astype(jnp.bfloat16)


def draw_kv_weight(key, part):
    key = jax.random.fold_in(key, 3)
    key_part = jnp.clip(jax.random.normal(jax.random.fold_in(key, 1), (D, KV_HEADS * HEAD_DIM), jnp.float32), -6.0, 6.0) * math.sqrt(3.0 / D)
    value_part = jnp.clip(jax.random.normal(jax.random.fold_in(key, 2), (D, KV_HEADS * HEAD_DIM), jnp.float32), -6.0, 6.0) * math.sqrt(1.0 / D)
    return jnp.concatenate([key_part, value_part], axis=1).astype(jnp.bfloat16)


def levels(rng, shape, cuts, low, top_value):
    loudness = 1.0
    for dim, parts in cuts:
        draws = jax.random.uniform(jax.random.fold_in(jax.random.fold_in(rng, 6), dim), (parts,), jnp.float32, low / len(cuts), top_value / len(cuts))
        loudness = loudness * jnp.repeat(jnp.exp(draws), shape[dim] // parts).reshape((-1,) + (1,) * (len(shape) - 1 - dim))
    return loudness


def bell_draw(stream_key, shape, scale, bound, cuts=(), held_as=jnp.bfloat16):
    entries = scale * jax.random.normal(stream_key, shape, jnp.float32)
    if cuts:
        entries = entries * levels(stream_key, shape, cuts, -0.22, 0.18)
    return jnp.clip(entries, -bound, bound).astype(held_as)


def setup_inputs(seed: int = 0) -> dict:
    seeds = jax.random.split(jax.random.key(seed), 10)
    hidden_state = draw_hidden_state(jax.random.fold_in(seeds[9], 71), 0)
    router_weight = jnp.clip(0.2 + 0.8 * jax.random.uniform(seeds[1], (TOKENS,), jnp.float32) ** levels(seeds[1], (TOKENS,), ((0, 64),), -0.2, 0.2), 0.2, 1.0)
    norm_gain = jnp.clip(1.0 + 0.1 * jax.random.normal(seeds[2], (D,), jnp.float32), 0.5, 1.5)
    query_weight = draw_query_weight(jax.random.fold_in(seeds[9], 71), 0)
    kv_weight = draw_kv_weight(jax.random.fold_in(seeds[9], 71), 0)
    out_weight = bell_draw(seeds[5], (HEADS * HEAD_DIM, D), (HEADS * HEAD_DIM) ** -0.5, 0.09375, ((0, 16),))
    sel_rows = draw_sel_rows(jax.random.fold_in(seeds[9], 71), 0)
    dest_shard = draw_dest_shard(jax.random.fold_in(seeds[9], 71), 0)
    dest_slot = draw_dest_slot(jax.random.fold_in(seeds[9], 71), 0)
    return dict(hidden_state=hidden_state, router_weight=router_weight, norm_gain=norm_gain, query_weight=query_weight, kv_weight=kv_weight, out_weight=out_weight, sel_rows=sel_rows, dest_shard=dest_shard, dest_slot=dest_slot)


rope_base = 500000.0

def rotate(head_vals, positions):
    half_dim = head_vals.shape[-1] // 2
    freqs = rope_base ** (-(jnp.arange(half_dim, dtype=jnp.float32) * 2.0 / head_vals.shape[-1]))
    angles = positions.astype(jnp.float32)[:, None] * freqs[None, :]
    cosine = jnp.cos(angles)[:, None, :]
    sine = jnp.sin(angles)[:, None, :]
    first_half = head_vals[..., :half_dim]
    second_half = head_vals[..., half_dim:]
    return jnp.concatenate([first_half * cosine - second_half * sine, second_half * cosine + first_half * sine], axis=-1)

def reference(hidden_state, router_weight, norm_gain, query_weight, kv_weight, out_weight, sel_rows, dest_shard, dest_slot):
    shard_of = jnp.arange(N_SEQ * SEL_CAP, dtype=jnp.int32) // SEL_CAP
    usable = sel_rows >= 0
    position = shard_of * TOK_DEV + jnp.maximum(sel_rows, 0)
    rank_order = dest_slot * N_SEQ + dest_shard
    target = jnp.where(usable, rank_order, SELECTED)
    by_rank = jnp.zeros((SELECTED,), jnp.int32).at[target].set(position, mode='drop')
    chosen = hidden_state[by_rank]
    row_float = chosen.astype(jnp.float32)
    inverse = lax.rsqrt(lax.optimization_barrier(jnp.mean(row_float * row_float, axis=1, keepdims=True)) + 1e-05)
    normed = (row_float * inverse * norm_gain[None, :]).astype(jnp.bfloat16)
    queries = jnp.dot(normed, query_weight, preferred_element_type=jnp.float32).reshape(SELECTED, HEADS, HEAD_DIM)
    queries = rotate(queries, by_rank).astype(jnp.bfloat16)
    key_value = jnp.dot(normed, kv_weight, preferred_element_type=jnp.float32)
    key_heads = key_value[:, :KV_HEADS * HEAD_DIM].reshape(SELECTED, KV_HEADS, HEAD_DIM)
    key_heads = rotate(key_heads, by_rank).astype(jnp.bfloat16)
    value_heads = key_value[:, KV_HEADS * HEAD_DIM:].reshape(SELECTED, KV_HEADS, HEAD_DIM).astype(jnp.bfloat16)
    query_major = queries.transpose(1, 0, 2)
    key_major = key_heads.transpose(1, 0, 2)
    value_major = value_heads.transpose(1, 0, 2)
    order_ids = jnp.arange(SELECTED, dtype=jnp.int32)
    causal = order_ids[:, None] >= order_ids[None, :]
    group_size = HEADS // KV_HEADS
    score_scale = 1.0 / math.sqrt(HEAD_DIM)

    def one_head(head_id):
        query_one = query_major[head_id]
        key_one = key_major[head_id // group_size]
        value_one = value_major[head_id // group_size]
        scores = jnp.dot(query_one, key_one.T, preferred_element_type=jnp.float32) * score_scale
        masked = jnp.where(causal, scores, -jnp.inf)
        row_max = lax.optimization_barrier(jnp.max(masked, axis=1, keepdims=True))
        weights = jnp.where(causal, jnp.exp(masked - row_max), 0.0)
        row_total = lax.optimization_barrier(jnp.sum(weights, axis=1, keepdims=True))
        return jnp.dot(weights.astype(jnp.bfloat16), value_one, preferred_element_type=jnp.float32) / row_total
    attended = lax.map(one_head, jnp.arange(HEADS, dtype=jnp.int32))
    attended = attended.transpose(1, 0, 2).reshape(SELECTED, HEADS * HEAD_DIM).astype(jnp.bfloat16)
    group_cols = HEADS * HEAD_DIM // N_MP

    def add_group(group_id, total_now):
        start = (jnp.asarray(group_id, jnp.int32) * group_cols).astype(jnp.int32)
        cols = lax.dynamic_slice_in_dim(attended, start, group_cols, 1)
        rows = lax.dynamic_slice_in_dim(out_weight, start, group_cols, 0)
        partial_sum = jnp.dot(cols, rows, preferred_element_type=jnp.float32).astype(jnp.bfloat16)
        partial_sum = lax.optimization_barrier(partial_sum)
        return total_now + partial_sum.astype(jnp.float32)
    summed = lax.fori_loop(0, N_MP, add_group, jnp.zeros((SELECTED, D), jnp.float32))
    update_rows = summed.astype(jnp.bfloat16)
    fresh = (row_float + router_weight[by_rank][:, None] * update_rows.astype(jnp.float32)).astype(jnp.bfloat16)
    return hidden_state.at[by_rank].set(fresh)
```

```python
import functools
import math

import jax
import jax.numpy as jnp
from jax import lax
from jax.experimental import pallas as pl
from jax.experimental.pallas import tpu as pltpu
from jax.sharding import Mesh
from jax.sharding import PartitionSpec as P

KV_HEADS = 8
HEAD_DIM = 128
ROPE_BASE = 500000.0
EPS = 1e-05

Z, X, Y, C = 16, 4, 8, 2
SEQ, MP = ("z", "x"), ("y", "c")
N_MP = Y * C
CAP = 128
TOK = 512
WIDTH = 256
EARLY = 112
LATE = CAP - EARLY
STATS = 16
UNUSED = 1e30
LOW, LOWER = -1e30, -2e30
VMEM = 48 * 1024 * 1024

params = pltpu.CompilerParams(vmem_limit_bytes=VMEM)
in_vmem = pl.BlockSpec(memory_space=pltpu.VMEM)
in_smem = pl.BlockSpec(memory_space=pltpu.SMEM)


def shape(dims, dtype=jnp.bfloat16):
    return jax.ShapeDtypeStruct(dims, dtype)


def dot(a, b, contract):
    return lax.dot_general(a, b, (contract, ((), ())), preferred_element_type=jnp.float32)


def one_hot(sel_row):
    rows = lax.broadcasted_iota(jnp.int32, (TOK, CAP), 0)
    return jnp.where(rows == sel_row, 1.0, 0.0)


def pick_kernel(sel_ref, hidden_ref, early_ref, late_ref):
    hot = one_hot(sel_ref[...]).astype(jnp.bfloat16)
    picked = dot(hot, hidden_ref[...], ((0,), (0,))).astype(jnp.bfloat16)
    early_ref[...] = picked[:EARLY]
    for m in range(N_MP):
        late_ref[m] = picked[EARLY:]


def norm_kv_kernel(
    early_ref, late_ref, gain_ref, weight_ref, cos_ref, sin_ref, mark_ref, normed_ref, kv_ref
):
    parts = ((early_ref, 0, EARLY), (late_ref, EARLY, LATE))
    for ref, first, count in parts:
        square = jnp.zeros((count, WIDTH), jnp.float32)
        for m in range(N_MP):
            vals = ref[m].astype(jnp.float32)
            square += vals * vals
        mean = jnp.sum(square, axis=1, keepdims=True) / (N_MP * WIDTH)
        inverse = lax.rsqrt(mean + EPS)
        for m in range(N_MP):
            vals = ref[m].astype(jnp.float32) * inverse * gain_ref[m : m + 1, :]
            normed_ref[m, first : first + count, :] = vals.astype(jnp.bfloat16)
    total = jnp.zeros((CAP, HEAD_DIM), jnp.float32)
    for m in range(N_MP):
        total += dot(normed_ref[m], weight_ref[m * WIDTH : (m + 1) * WIDTH, :], ((1,), (0,)))
    turned = total * cos_ref[...] + pltpu.roll(total, HEAD_DIM // 2, 1) * sin_ref[...]
    kv_ref[...] = (turned + mark_ref[...]).astype(jnp.bfloat16)


def query_kernel(normed_ref, weight_ref, cos_ref, sin_ref, out_ref):
    total = jnp.zeros((CAP, WIDTH), jnp.float32)
    for m in range(N_MP):
        total += dot(normed_ref[m], weight_ref[m * WIDTH : (m + 1) * WIDTH, :], ((1,), (0,)))
    for h in range(WIDTH // HEAD_DIM):
        head = total[:, h * HEAD_DIM : (h + 1) * HEAD_DIM]
        turned = head * cos_ref[...] + pltpu.roll(head, HEAD_DIM // 2, 1) * sin_ref[...]
        turned = turned.astype(jnp.bfloat16)
        for t in range(X):
            out_ref[t, :, h * HEAD_DIM : (h + 1) * HEAD_DIM] = turned


def attend_kernel(place_ref, query_ref, own_ref, other_ref, out_ref, high_ref, sum_ref, acc_ref):
    z, x, c = place_ref[0], place_ref[1], place_ref[2]
    heads = WIDTH // HEAD_DIM
    queries = X * CAP
    scale = math.log2(math.e) / math.sqrt(HEAD_DIM)
    high_ref[...] = jnp.full(high_ref.shape, LOW, jnp.float32)
    sum_ref[...] = jnp.zeros(sum_ref.shape, jnp.float32)
    acc_ref[...] = jnp.zeros(acc_ref.shape, jnp.float32)
    query_order = z * (X * CAP) + lax.broadcasted_iota(jnp.int32, (1, queries), 1)

    def step(pair, carry):
        own = own_ref[pl.ds(2 * pair, 2)].reshape(2 * CAP, HEAD_DIM)
        other = other_ref[pl.ds(2 * pair, 2)].reshape(2 * CAP, HEAD_DIM)
        keys = jnp.where(c == 0, own, other)
        values = jnp.where(c == 0, other, own)
        values_t = values.T
        row = lax.broadcasted_iota(jnp.int32, (2 * CAP, 1), 0)
        shard = (2 * pair + row // CAP) * X + x
        key_order = shard * CAP + row % CAP
        unused = keys[:, 0:1].astype(jnp.float32) > 0.1 * UNUSED
        key_order = jnp.where(unused, 1 << 30, key_order)
        allowed = key_order <= query_order
        for h in range(heads):
            query = query_ref[:, :, h * HEAD_DIM : (h + 1) * HEAD_DIM].reshape(queries, HEAD_DIM)
            scores = dot(keys, query, ((1,), (1,))) * scale
            scores = jnp.where(allowed, scores, LOWER)
            before = high_ref[h]
            high = jnp.maximum(before, jnp.max(scores, axis=0, keepdims=True))
            weights = jnp.exp2(scores - high)
            fade = jnp.exp2(before - high)
            high_ref[h] = high
            sum_ref[h] = sum_ref[h] * fade + jnp.sum(weights, axis=0, keepdims=True)
            acc_ref[h] = acc_ref[h] * fade + dot(
                values_t, weights.astype(jnp.bfloat16), ((1,), (0,))
            )
        return carry

    lax.fori_loop(0, z // 2 + 1, step, 0)
    stat_row = lax.broadcasted_iota(jnp.int32, (STATS, queries), 0)
    stats = jnp.zeros((STATS, queries), jnp.float32)
    for h in range(heads):
        total = sum_ref[h]
        safe = jnp.maximum(total, 1e-30)
        attended = (acc_ref[h] / safe).astype(jnp.bfloat16)
        for t in range(X):
            out_ref[t, h * HEAD_DIM : (h + 1) * HEAD_DIM, :] = attended[:, t * CAP : (t + 1) * CAP]
        left = jnp.where(total > 0.0, high_ref[h] + jnp.log2(safe), LOW)
        for k in range(3):
            piece = left.astype(jnp.bfloat16).astype(jnp.float32)
            stats = jnp.where(stat_row == heads * k + h, piece, stats)
            left = left - piece
    stats = stats.astype(jnp.bfloat16)
    for t in range(X):
        out_ref[t, heads * HEAD_DIM :, :] = stats[:, t * CAP : (t + 1) * CAP]


def project_kernel(parts_ref, weight_ref, out_ref):
    heads = WIDTH // HEAD_DIM
    stats = [parts_ref[t, heads * HEAD_DIM :, :].astype(jnp.float32) for t in range(X)]
    columns = []
    for h in range(heads):
        logs = [s[h : h + 1] + s[heads + h : heads + h + 1] + s[2 * heads + h : 2 * heads + h + 1] for s in stats]
        high = functools.reduce(jnp.maximum, logs)
        shares = [jnp.exp2(v - high) for v in logs]
        total = functools.reduce(jnp.add, shares)
        mixed = jnp.zeros((HEAD_DIM, CAP), jnp.float32)
        for t in range(X):
            part = parts_ref[t, h * HEAD_DIM : (h + 1) * HEAD_DIM, :].astype(jnp.float32)
            mixed += part * shares[t]
        columns.append((mixed / total).T.astype(jnp.bfloat16))
    attended = jnp.concatenate(columns, axis=1)
    for m in range(N_MP):
        block = dot(attended, weight_ref[:, m * WIDTH : (m + 1) * WIDTH], ((1,), (0,)))
        out_ref[m] = block.astype(jnp.bfloat16)


def mix_kernel(sel_ref, router_ref, hidden_ref, parts_ref, out_ref):
    update = jnp.zeros((CAP, WIDTH), jnp.float32)
    for m in range(N_MP):
        update += parts_ref[m].astype(jnp.float32)
    hot = one_hot(sel_ref[...])
    spread = dot(hot.astype(jnp.bfloat16), update.astype(jnp.bfloat16), ((1,), (0,)))
    taken = jnp.max(hot, axis=1, keepdims=True) > 0.0
    eye = lax.broadcasted_iota(jnp.int32, (CAP, CAP), 0) == lax.broadcasted_iota(
        jnp.int32, (CAP, CAP), 1
    )
    for b in range(TOK // CAP):
        rows = slice(b * CAP, (b + 1) * CAP)
        router = jnp.sum(
            jnp.where(eye, router_ref[:, rows], 0.0), axis=1, keepdims=True
        )
        before = hidden_ref[rows, :]
        fresh = before.astype(jnp.float32) + router * spread[rows]
        out_ref[rows, :] = jnp.where(taken[rows], fresh, before.astype(jnp.float32)).astype(
            jnp.bfloat16
        )


def call(kernel, out_shape, count, scratch=(), smem_first=False, flops=0, nbytes=0):
    specs = [in_vmem] * count
    if smem_first:
        specs[0] = in_smem
    many = isinstance(out_shape, (tuple, list))
    return pl.pallas_call(
        kernel,
        out_shape=out_shape,
        in_specs=specs,
        out_specs=[in_vmem] * len(out_shape) if many else in_vmem,
        scratch_shapes=list(scratch),
        compiler_params=params,
        cost_estimate=pl.CostEstimate(flops=flops, bytes_accessed=nbytes, transcendentals=0),
    )


def local(
    hidden_state,
    router_weight,
    norm_gain,
    query_weight,
    kv_weight,
    out_weight,
    sel_rows,
    dest_shard,
    dest_slot,
):
    z, x = lax.axis_index("z"), lax.axis_index("x")
    core = lax.axis_index("c")
    model = lax.axis_index("y") * C + core
    place = jnp.stack([z, x, core]).astype(jnp.int32)
    sel = sel_rows.reshape(1, CAP)

    with jax.named_scope("pick"):
        early, late = call(
            pick_kernel, [shape((EARLY, WIDTH)), shape((N_MP, LATE, WIDTH))], 2
        )(sel, hidden_state)
    with jax.named_scope("gather_features"):
        late_all = lax.all_to_all(late, MP, 0, 0, tiled=True)
        early_all = lax.all_gather(early, MP, axis=0, tiled=False)

    with jax.named_scope("rotation"):
        half = HEAD_DIM // 2
        positions = (z * X + x) * TOK + jnp.maximum(sel_rows, 0)
        freqs = ROPE_BASE ** (-(jnp.arange(half, dtype=jnp.float32) * 2.0 / HEAD_DIM))
        angles = positions.astype(jnp.float32)[:, None] * freqs[None, :]
        cosine, sine = jnp.cos(angles), jnp.sin(angles)
        cos_q = jnp.concatenate([cosine, cosine], axis=1)
        sin_q = jnp.concatenate([-sine, sine], axis=1)
        is_key = model < KV_HEADS
        cos_kv = jnp.where(is_key, cos_q, 1.0)
        sin_kv = jnp.where(is_key, sin_q, 0.0)
        lane = jnp.arange(HEAD_DIM, dtype=jnp.int32)[None, :]
        mark = jnp.where(is_key & (sel_rows < 0)[:, None] & (lane == 0), UNUSED, 0.0)

    with jax.named_scope("keys_values"):
        normed, kv = call(
            norm_kv_kernel,
            [shape((N_MP, CAP, WIDTH)), shape((CAP, HEAD_DIM))],
            7,
            flops=2 * CAP * 4096 * HEAD_DIM,
            nbytes=4 << 20,
        )(early_all, late_all, norm_gain.reshape(N_MP, WIDTH), kv_weight, cos_kv, sin_kv, mark)
        to_heads = [(m, 2 * m if m < KV_HEADS else 2 * (m - KV_HEADS) + 1) for m in range(N_MP)]
        kv = lax.ppermute(kv, MP, to_heads)
    with jax.named_scope("queries"):
        queries = call(
            query_kernel,
            shape((X, CAP, WIDTH)),
            4,
            flops=2 * CAP * 4096 * WIDTH,
            nbytes=4 << 20,
        )(normed, query_weight, cos_q, sin_q)
        queries = lax.all_to_all(queries, "x", 0, 0, tiled=True)
    with jax.named_scope("spread_keys_values"):
        own = lax.all_to_all(jnp.broadcast_to(kv[None], (Z, CAP, HEAD_DIM)), "z", 0, 0, tiled=True)
        other = lax.ppermute(own, "c", [(0, 1), (1, 0)])
    with jax.named_scope("attend"):
        heads = WIDTH // HEAD_DIM
        parts = call(
            attend_kernel,
            shape((X, WIDTH + STATS, CAP)),
            4,
            scratch=(
                pltpu.VMEM((heads, 1, X * CAP), jnp.float32),
                pltpu.VMEM((heads, 1, X * CAP), jnp.float32),
                pltpu.VMEM((heads, HEAD_DIM, X * CAP), jnp.float32),
            ),
            smem_first=True,
            flops=4 * X * CAP * WIDTH * Z * CAP,
            nbytes=2 << 20,
        )(place, queries, own, other)
        parts = lax.all_to_all(parts, "x", 0, 0, tiled=True)
    with jax.named_scope("project"):
        partial = call(
            project_kernel,
            shape((N_MP, CAP, WIDTH)),
            2,
            flops=2 * CAP * WIDTH * 4096,
            nbytes=3 << 20,
        )(parts, out_weight)
        partial = lax.all_to_all(partial, MP, 0, 0, tiled=True)
    with jax.named_scope("mix"):
        return call(mix_kernel, shape((TOK, WIDTH)), 4, nbytes=2 << 20)(
            sel, router_weight.reshape(1, TOK), hidden_state, partial
        )


def solution(mesh):
    fine = Mesh(mesh.devices.reshape(Z, X, Y, C), ("z", "x", "y", "c"))
    in_specs = (
        P(SEQ, MP),
        P(SEQ),
        P(),
        P(None, MP),
        P(None, MP),
        P(MP, None),
        P(SEQ),
        P(SEQ),
        P(SEQ),
    )
    return jax.shard_map(
        local, mesh=fine, in_specs=in_specs, out_specs=P(SEQ, MP), check_vma=False
    )
```

```python
import functools
import math

import jax
import jax.numpy as jnp
from jax import lax
from jax.experimental import pallas as pl
from jax.experimental.pallas import tpu as pltpu
from jax.sharding import Mesh
from jax.sharding import PartitionSpec as P

HEAD_DIM = 128
HALF_DIM = HEAD_DIM // 2
ROPE_BASE = 500000.0
EPS = 1e-05

Z, X, Y, C = 16, 4, 8, 2
AXES = ("z", "x", "y", "c")
SEQ, MP = ("z", "x"), ("y", "c")
N_MP = Y * C
CAP = 128
HALF = CAP // C
TOK = 512
WIDTH = 256
HEADS = WIDTH // HEAD_DIM
ROWS = C * HEADS * HALF
STATS = 16
UNUSED = 1e30
CHAINS = 2
LOW, LOWER = -1e30, -2e30
VMEM = 48 * 1024 * 1024
WHOLE = 62 * 1024 * 1024

in_vmem = pl.BlockSpec(memory_space=pltpu.VMEM)
in_smem = pl.BlockSpec(memory_space=pltpu.SMEM)
in_hbm = pl.BlockSpec(memory_space=pltpu.HBM)


def shape(dims, dtype=jnp.bfloat16):
    return jax.ShapeDtypeStruct(dims, dtype)


def dot(a, b, contract):
    return lax.dot_general(a, b, (contract, ((), ())), preferred_element_type=jnp.float32)


def one_hot(sel_row):
    rows = lax.broadcasted_iota(jnp.int32, (TOK, CAP), 0)
    return jnp.where(rows == sel_row, 1.0, 0.0)


def turn(head, cosine, sine):
    return head * cosine + pltpu.roll(head, HALF_DIM, 1) * sine


def pick_kernel(sel_ref, hidden_ref, out_ref):
    hot = one_hot(sel_ref[...]).astype(jnp.bfloat16)
    picked = dot(hot, hidden_ref[...], ((0,), (0,))).astype(jnp.bfloat16)
    for m in range(N_MP):
        half = m % C
        out_ref[m] = picked[half * HALF : (half + 1) * HALF]


def touch_kernel(weight_ref, after_ref, out_ref):
    del after_ref
    out_ref[...] = weight_ref[:16, :]


def norm_kv_kernel(
    core_ref,
    own_ref,
    other_ref,
    gain_ref,
    cos_ref,
    sin_ref,
    mark_ref,
    weight_ref,
    after_ref,
    normed_ref,
    kv_ref,
):
    del after_ref
    core = core_ref[0]
    for ref, half in ((own_ref, core), (other_ref, 1 - core)):
        square = jnp.zeros((HALF, WIDTH), jnp.float32)
        for m in range(N_MP):
            vals = ref[m].astype(jnp.float32)
            square += vals * vals
        mean = jnp.sum(square, axis=1, keepdims=True) / (N_MP * WIDTH)
        inverse = lax.rsqrt(mean + EPS)
        first = pl.multiple_of(half * HALF, HALF)
        for m in range(N_MP):
            vals = ref[m].astype(jnp.float32) * inverse * gain_ref[m : m + 1, :]
            normed_ref[pl.ds(first, HALF), m * WIDTH : (m + 1) * WIDTH] = vals.astype(jnp.bfloat16)
    total = dot(normed_ref[...], weight_ref[...], ((1,), (0,)))
    kv_ref[...] = (turn(total, cos_ref[...], sin_ref[...]) + mark_ref[...]).astype(jnp.bfloat16)


def query_kernel(core_ref, normed_ref, cos_ref, sin_ref, weight_ref, mine_ref, theirs_ref):
    core = core_ref[0]
    total = dot(normed_ref[...], weight_ref[...], ((1,), (0,)))
    for h in range(HEADS):
        head = total[:, h * HEAD_DIM : (h + 1) * HEAD_DIM]
        turned = turn(head, cos_ref[...], sin_ref[...]).astype(jnp.bfloat16)
        lower, upper = turned[:HALF], turned[HALF:]
        rows = slice(h * HALF, (h + 1) * HALF)
        mine_ref[rows, :] = jnp.where(core == 0, lower, upper)
        theirs_ref[rows, :] = jnp.where(core == 0, upper, lower)


def attend_kernel(place_ref, query_ref, own_ref, other_ref, out_ref, high_ref, sum_ref, acc_ref):
    z, x, c = place_ref[0], place_ref[1], place_ref[2]
    columns = X * ROWS
    scale = math.log2(math.e) / math.sqrt(HEAD_DIM)
    high_ref[...] = jnp.full(high_ref.shape, LOW, jnp.float32)
    sum_ref[...] = jnp.zeros(sum_ref.shape, jnp.float32)
    acc_ref[...] = jnp.zeros(acc_ref.shape, jnp.float32)
    column = lax.broadcasted_iota(jnp.int32, (1, columns), 1)
    query_shard = z * X + column // ROWS
    query_order = query_shard * CAP + c * HALF + column % HALF

    def step(pair, carry):
        own = own_ref[pl.ds(2 * pair, 2)].reshape(2 * CAP, HEAD_DIM)
        other = other_ref[pl.ds(2 * pair, 2)].reshape(2 * CAP, HEAD_DIM)
        keys = jnp.where(c == 0, own, other)
        values_t = jnp.where(c == 0, other, own).T
        row = lax.broadcasted_iota(jnp.int32, (2 * CAP, 1), 0)
        shard = (2 * pair + row // CAP) * X + x
        key_order = shard * CAP + row % CAP
        unused = keys[:, 0:1].astype(jnp.float32) > 0.1 * UNUSED
        key_order = jnp.where(unused, 1 << 30, key_order)
        for part in range(CHAINS):
            span = slice(part * columns // CHAINS, (part + 1) * columns // CHAINS)
            scores = dot(keys, query_ref[span, :], ((1,), (1,))) * scale
            scores = jnp.where(key_order <= query_order[:, span], scores, LOWER)
            before = high_ref[:, span]
            high = jnp.maximum(before, jnp.max(scores, axis=0, keepdims=True))
            weights = jnp.exp2(scores - high)
            fade = jnp.exp2(before - high)
            high_ref[:, span] = high
            sum_ref[:, span] = sum_ref[:, span] * fade + jnp.sum(weights, axis=0, keepdims=True)
            acc_ref[:, span] = acc_ref[:, span] * fade + dot(
                values_t, weights.astype(jnp.bfloat16), ((1,), (0,))
            )
        return carry

    lax.fori_loop(0, z // 2 + 1, step, 0)
    total = sum_ref[...]
    safe = jnp.maximum(total, 1e-30)
    attended = (acc_ref[...] / safe).astype(jnp.bfloat16)
    stat_row = lax.broadcasted_iota(jnp.int32, (STATS, columns), 0)
    stats = jnp.zeros((STATS, columns), jnp.float32)
    left = jnp.where(total > 0.0, high_ref[...] + jnp.log2(safe), LOW)
    for k in range(3):
        piece = left.astype(jnp.bfloat16).astype(jnp.float32)
        stats = jnp.where(stat_row == k, piece, stats)
        left = left - piece
    stats = stats.astype(jnp.bfloat16)
    for home in range(X):
        span = slice(home * ROWS, (home + 1) * ROWS)
        out_ref[home, :HEAD_DIM, :] = attended[:, span]
        out_ref[home, HEAD_DIM:, :] = stats[:, span]


def project_kernel(parts_ref, other_ref, own_ref, out_ref, own_buf, arrived):
    copy = pltpu.make_async_copy(own_ref, own_buf, arrived)
    copy.start()
    logs = []
    for t in range(X):
        stats = parts_ref[t, HEAD_DIM:, :].astype(jnp.float32)
        logs.append(stats[0:1] + stats[1:2] + stats[2:3])
    high = functools.reduce(jnp.maximum, logs)
    shares = [jnp.exp2(v - high) for v in logs]
    total = functools.reduce(jnp.add, shares)
    merged = jnp.zeros((HEAD_DIM, ROWS), jnp.float32)
    for t in range(X):
        part = parts_ref[t, :HEAD_DIM, :].astype(jnp.float32)
        merged += part * (shares[t] / total)
    merged = merged.T.astype(jnp.bfloat16)
    attended = jnp.concatenate(
        [merged[j * HALF : (j + 1) * HALF] for j in range(C * HEADS)], axis=1
    )
    copy.wait()
    for m in range(N_MP):
        columns = slice(m * WIDTH, (m + 1) * WIDTH)
        block = dot(attended[:, :WIDTH], own_buf[:, columns], ((1,), (0,)))
        block += dot(attended[:, WIDTH:], other_ref[:, columns], ((1,), (0,)))
        out_ref[m] = block.astype(jnp.bfloat16)


def mix_kernel(sel_ref, router_ref, hidden_ref, parts_ref, out_ref):
    halves = []
    for half in range(C):
        update = jnp.zeros((HALF, WIDTH), jnp.float32)
        for y in range(Y):
            update += parts_ref[y * C + half].astype(jnp.float32)
        halves.append(update.astype(jnp.bfloat16))
    hot = one_hot(sel_ref[...])
    spread = dot(hot.astype(jnp.bfloat16), jnp.concatenate(halves, axis=0), ((1,), (0,)))
    taken = jnp.max(hot, axis=1, keepdims=True) > 0.0
    eye = lax.broadcasted_iota(jnp.int32, (CAP, CAP), 0) == lax.broadcasted_iota(
        jnp.int32, (CAP, CAP), 1
    )
    for b in range(TOK // CAP):
        rows = slice(b * CAP, (b + 1) * CAP)
        router = jnp.sum(jnp.where(eye, router_ref[:, rows], 0.0), axis=1, keepdims=True)
        before = hidden_ref[rows, :].astype(jnp.float32)
        fresh = before + router * spread[rows]
        out_ref[rows, :] = jnp.where(taken[rows], fresh, before).astype(jnp.bfloat16)


def call(kernel, out_shape, count, scratch=(), smem_first=False, loose=0, flops=0, nbytes=0, vmem=VMEM):
    specs = [in_vmem] * (count - loose) + [in_hbm] * loose
    if smem_first:
        specs[0] = in_smem
    many = isinstance(out_shape, (tuple, list))
    return pl.pallas_call(
        kernel,
        out_shape=out_shape,
        in_specs=specs,
        out_specs=[in_vmem] * len(out_shape) if many else in_vmem,
        scratch_shapes=list(scratch),
        compiler_params=pltpu.CompilerParams(vmem_limit_bytes=vmem),
        cost_estimate=pl.CostEstimate(flops=flops, bytes_accessed=nbytes, transcendentals=0),
    )


def local(
    hidden_state,
    router_weight,
    norm_gain,
    query_weight,
    kv_weight,
    out_weight,
    sel_rows,
    dest_shard,
    dest_slot,
):
    z, x = lax.axis_index("z"), lax.axis_index("x")
    y, core = lax.axis_index("y"), lax.axis_index("c")
    is_key = y < Y // 2
    place = jnp.stack([z, x, core]).astype(jnp.int32)
    core_at = core.astype(jnp.int32)[None]
    sel = sel_rows.reshape(1, CAP)
    swap = [(0, 1), (1, 0)]

    with jax.named_scope("pick"):
        picked = call(pick_kernel, shape((N_MP, HALF, WIDTH)), 2, vmem=WHOLE)(sel, hidden_state)
    with jax.named_scope("gather_features"):
        own_rows = lax.all_to_all(picked, MP, 0, 0, tiled=True)
        other_rows = lax.ppermute(own_rows, "c", swap)

    with jax.named_scope("rotation"):
        positions = (z * X + x) * TOK + jnp.maximum(sel_rows, 0)
        freqs = ROPE_BASE ** (-(jnp.arange(HALF_DIM, dtype=jnp.float32) * 2.0 / HEAD_DIM))
        angles = positions.astype(jnp.float32)[:, None] * freqs[None, :]
        cosine, sine = jnp.cos(angles), jnp.sin(angles)
        cos_q = jnp.concatenate([cosine, cosine], axis=1)
        sin_q = jnp.concatenate([-sine, sine], axis=1)
        cos_kv = jnp.where(is_key, cos_q, 1.0)
        sin_kv = jnp.where(is_key, sin_q, 0.0)
        lane = jnp.arange(HEAD_DIM, dtype=jnp.int32)[None, :]
        mark = jnp.where(is_key & (sel_rows < 0)[:, None] & (lane == 0), UNUSED, 0.0)

    with jax.named_scope("keys_values"):
        touched = call(touch_kernel, shape((16, HEAD_DIM)), 2, loose=1)(kv_weight, picked)
        normed, kv = call(
            norm_kv_kernel,
            [shape((CAP, N_MP * WIDTH)), shape((CAP, HEAD_DIM))],
            9,
            smem_first=True,
            flops=2 * CAP * N_MP * WIDTH * HEAD_DIM,
            nbytes=3 << 20,
        )(
            core_at,
            own_rows,
            other_rows,
            norm_gain.reshape(N_MP, WIDTH),
            cos_kv,
            sin_kv,
            mark,
            kv_weight,
            touched,
        )
        to_heads = [(m, 2 * m if m < Y else 2 * (m - Y) + 1) for m in range(N_MP)]
        kv = lax.ppermute(kv, MP, to_heads)
    with jax.named_scope("queries"):
        mine, theirs = call(
            query_kernel,
            [shape((HEADS * HALF, HEAD_DIM)), shape((HEADS * HALF, HEAD_DIM))],
            5,
            smem_first=True,
            flops=2 * CAP * N_MP * WIDTH * WIDTH,
            nbytes=3 << 20,
        )(core_at, normed, cos_q, sin_q, query_weight)
        kv, mine = lax.optimization_barrier((kv, mine))
    with jax.named_scope("spread_keys_values"):
        kv = jnp.broadcast_to(kv[None], (Z, CAP, HEAD_DIM))
        kv, theirs = lax.optimization_barrier((kv, theirs))
        own = lax.all_to_all(kv, "z", 0, 0, tiled=True)
    with jax.named_scope("share_queries"):
        queries = jnp.concatenate([mine, lax.ppermute(theirs, "c", swap)], axis=0)
        queries = lax.all_gather(queries, "x", axis=0, tiled=True)
        own, queries = lax.optimization_barrier((own, queries))
        other = lax.ppermute(own, "c", swap)
    out_other = lax.ppermute(out_weight, "c", swap)
    with jax.named_scope("attend"):
        columns = X * ROWS
        parts = call(
            attend_kernel,
            shape((X, HEAD_DIM + STATS, ROWS)),
            4,
            scratch=(
                pltpu.VMEM((1, columns), jnp.float32),
                pltpu.VMEM((1, columns), jnp.float32),
                pltpu.VMEM((HEAD_DIM, columns), jnp.float32),
            ),
            smem_first=True,
            flops=4 * columns * HEAD_DIM * Z * CAP,
            nbytes=2 << 20,
        )(place, queries, own, other)
        parts = lax.all_to_all(parts, "x", 0, 0, tiled=True)
    with jax.named_scope("project"):
        partial = call(
            project_kernel,
            shape((N_MP, HALF, WIDTH)),
            3,
            loose=1,
            scratch=(
                pltpu.VMEM((WIDTH, N_MP * WIDTH), jnp.bfloat16),
                pltpu.SemaphoreType.DMA,
            ),
            flops=2 * CAP * WIDTH * N_MP * WIDTH,
            nbytes=5 << 20,
        )(parts, out_other, out_weight)
        partial = lax.all_to_all(partial, MP, 0, 0, tiled=True)
    with jax.named_scope("mix"):
        return call(mix_kernel, shape((TOK, WIDTH)), 4, nbytes=2 << 20)(
            sel, router_weight.reshape(1, TOK), hidden_state, partial
        )


def solution(mesh):
    fine = Mesh(mesh.devices.reshape(Z, X, Y, C), AXES)
    in_specs = (
        P(SEQ, MP),
        P(SEQ),
        P(),
        P(None, MP),
        P(None, MP),
        P(MP, None),
        P(SEQ),
        P(SEQ),
        P(SEQ),
    )
    return jax.shard_map(
        local, mesh=fine, in_specs=in_specs, out_specs=P(SEQ, MP), check_vma=False
    )
```

```python
import functools
import math

import jax
import jax.numpy as jnp
from jax import lax
from jax.experimental import pallas as pl
from jax.experimental.pallas import tpu as pltpu
from jax.sharding import Mesh
from jax.sharding import PartitionSpec as P

HEAD_DIM = 128
HALF_DIM = HEAD_DIM // 2
ROPE_BASE = 500000.0
EPS = 1e-05

ZH, ZP, X, Y, C = 8, 2, 4, 8, 2
AXES = ("zh", "zp", "x", "y", "c")
SEQ, MP = ("zh", "zp", "x"), ("y", "c")
NEAR = ("zp", "x")
GROUP = ZP * X
N_MP = Y * C
CAP = 128
HALF = CAP // C
TOK = 512
WIDTH = 256
HEADS = WIDTH // HEAD_DIM
ROWS = C * HEADS * HALF
STATS = 16
UNUSED = 1e30
PIECES = 4
CHAINS = 1
LOW, LOWER = -1e30, -2e30
VMEM = 48 * 1024 * 1024
WHOLE = 62 * 1024 * 1024

in_vmem = pl.BlockSpec(memory_space=pltpu.VMEM)
in_smem = pl.BlockSpec(memory_space=pltpu.SMEM)
in_hbm = pl.BlockSpec(memory_space=pltpu.HBM)


def shape(dims, dtype=jnp.bfloat16):
    return jax.ShapeDtypeStruct(dims, dtype)


def dot(a, b, contract):
    return lax.dot_general(a, b, (contract, ((), ())), preferred_element_type=jnp.float32)


def one_hot(sel_row):
    rows = lax.broadcasted_iota(jnp.int32, (TOK, CAP), 0)
    return jnp.where(rows == sel_row, 1.0, 0.0)


def turn(head, cosine, sine):
    return head * cosine + pltpu.roll(head, HALF_DIM, 1) * sine


def pick_kernel(sel_ref, hidden_ref, out_ref):
    hot = one_hot(sel_ref[...]).astype(jnp.bfloat16)
    picked = dot(hot, hidden_ref[...], ((0,), (0,))).astype(jnp.bfloat16)
    for m in range(N_MP):
        half = m % C
        out_ref[m] = picked[half * HALF : (half + 1) * HALF]


def touch_kernel(weight_ref, after_ref, out_ref):
    del after_ref
    out_ref[...] = weight_ref[:16, :HEAD_DIM]


def norm_kv_kernel(
    core_ref,
    own_ref,
    other_ref,
    gain_ref,
    cos_ref,
    sin_ref,
    mark_ref,
    weight_ref,
    after_ref,
    normed_ref,
    kv_ref,
):
    del after_ref
    core = core_ref[0]
    for ref, half in ((own_ref, core), (other_ref, 1 - core)):
        square = jnp.zeros((HALF, WIDTH), jnp.float32)
        for m in range(N_MP):
            vals = ref[m].astype(jnp.float32)
            square += vals * vals
        mean = jnp.sum(square, axis=1, keepdims=True) / (N_MP * WIDTH)
        inverse = lax.rsqrt(mean + EPS)
        first = pl.multiple_of(half * HALF, HALF)
        for m in range(N_MP):
            vals = ref[m].astype(jnp.float32) * inverse * gain_ref[m : m + 1, :]
            normed_ref[pl.ds(first, HALF), m * WIDTH : (m + 1) * WIDTH] = vals.astype(jnp.bfloat16)
    total = dot(normed_ref[...], weight_ref[...], ((1,), (0,)))
    kv_ref[...] = (turn(total, cos_ref[...], sin_ref[...]) + mark_ref[...]).astype(jnp.bfloat16)


def query_kernel(core_ref, normed_ref, cos_ref, sin_ref, weight_ref, mine_ref, theirs_ref):
    core = core_ref[0]
    total = dot(normed_ref[...], weight_ref[...], ((1,), (0,)))
    for h in range(HEADS):
        head = total[:, h * HEAD_DIM : (h + 1) * HEAD_DIM]
        turned = turn(head, cos_ref[...], sin_ref[...]).astype(jnp.bfloat16)
        lower, upper = turned[:HALF], turned[HALF:]
        rows = slice(h * HALF, (h + 1) * HALF)
        mine_ref[rows, :] = jnp.where(core == 0, lower, upper)
        theirs_ref[rows, :] = jnp.where(core == 0, upper, lower)


def attend_kernel(place_ref, query_ref, own_ref, other_ref, out_ref, high_ref, sum_ref, acc_ref):
    zh, zp, x, c = place_ref[0], place_ref[1], place_ref[2], place_ref[3]
    columns = GROUP * ROWS
    scale = math.log2(math.e) / math.sqrt(HEAD_DIM)
    high_ref[...] = jnp.full(high_ref.shape, LOW, jnp.float32)
    sum_ref[...] = jnp.zeros(sum_ref.shape, jnp.float32)
    acc_ref[...] = jnp.zeros(acc_ref.shape, jnp.float32)
    column = lax.broadcasted_iota(jnp.int32, (1, columns), 1)
    swapped = column // ROWS % ZP
    query_zp = zp + swapped - 2 * zp * swapped
    query_shard = (zh * ZP + query_zp) * X + column // (ZP * ROWS)
    query_order = query_shard * CAP + c * HALF + column % HALF

    def step(pair, carry):
        own = own_ref[pl.ds(2 * pair, 2)].reshape(2 * CAP, HEAD_DIM)
        other = other_ref[pl.ds(2 * pair, 2)].reshape(2 * CAP, HEAD_DIM)
        keys = jnp.where(c == 0, own, other)
        values_t = jnp.where(c == 0, other, own).T
        row = lax.broadcasted_iota(jnp.int32, (2 * CAP, 1), 0)
        shard = ((2 * pair + row // CAP) * ZP + zp) * X + x
        key_order = shard * CAP + row % CAP
        unused = keys[:, 0:1].astype(jnp.float32) > 0.1 * UNUSED
        key_order = jnp.where(unused, 1 << 30, key_order)
        for part in range(CHAINS):
            span = slice(part * columns // CHAINS, (part + 1) * columns // CHAINS)
            scores = dot(keys, query_ref[span, :], ((1,), (1,))) * scale
            scores = jnp.where(key_order <= query_order[:, span], scores, LOWER)
            before = high_ref[:, span]
            high = jnp.maximum(before, jnp.max(scores, axis=0, keepdims=True))
            weights = jnp.exp2(scores - high)
            fade = jnp.exp2(before - high)
            high_ref[:, span] = high
            sum_ref[:, span] = sum_ref[:, span] * fade + jnp.sum(weights, axis=0, keepdims=True)
            acc_ref[:, span] = acc_ref[:, span] * fade + dot(
                values_t, weights.astype(jnp.bfloat16), ((1,), (0,))
            )
        return carry

    lax.fori_loop(0, zh // 2 + 1, step, 0)
    total = sum_ref[...]
    safe = jnp.maximum(total, 1e-30)
    attended = (acc_ref[...] / safe).astype(jnp.bfloat16)
    stat_row = lax.broadcasted_iota(jnp.int32, (STATS, columns), 0)
    stats = jnp.zeros((STATS, columns), jnp.float32)
    left = jnp.where(total > 0.0, high_ref[...] + jnp.log2(safe), LOW)
    for k in range(3):
        piece = left.astype(jnp.bfloat16).astype(jnp.float32)
        stats = jnp.where(stat_row == k, piece, stats)
        left = left - piece
    stats = stats.astype(jnp.bfloat16)
    for to_x in range(X):
        for swap in range(ZP):
            first = (to_x * ZP + swap) * ROWS
            home = (zp + swap - 2 * zp * swap) * X + to_x
            out_ref[home, :HEAD_DIM, :] = attended[:, first : first + ROWS]
            out_ref[home, HEAD_DIM:, :] = stats[:, first : first + ROWS]


def project_kernel(parts_ref, own_ref, *refs):
    other_refs, (out_ref, other_buf, total_ref, arrived) = refs[:PIECES], refs[PIECES:]
    copies = [
        pltpu.make_async_copy(ref, other_buf.at[i], arrived.at[i])
        for i, ref in enumerate(other_refs)
    ]
    for copy in copies:
        copy.start()
    logs = []
    for t in range(GROUP):
        stats = parts_ref[t, HEAD_DIM:, :].astype(jnp.float32)
        logs.append(stats[0:1] + stats[1:2] + stats[2:3])
    high = functools.reduce(jnp.maximum, logs)
    shares = [jnp.exp2(v - high) for v in logs]
    total = functools.reduce(jnp.add, shares)
    merged = jnp.zeros((HEAD_DIM, ROWS), jnp.float32)
    for t in range(GROUP):
        part = parts_ref[t, :HEAD_DIM, :].astype(jnp.float32)
        merged += part * (shares[t] / total)
    merged = merged.T.astype(jnp.bfloat16)
    attended = jnp.concatenate(
        [merged[j * HALF : (j + 1) * HALF] for j in range(C * HEADS)], axis=1
    )
    for m in range(N_MP):
        columns = slice(m * WIDTH, (m + 1) * WIDTH)
        total_ref[m] = dot(attended[:, :WIDTH], own_ref[:, columns], ((1,), (0,)))
    for copy in copies:
        copy.wait()
    for m in range(N_MP):
        columns = slice(m * WIDTH, (m + 1) * WIDTH)
        block = total_ref[m]
        for i in range(PIECES):
            rows = slice(WIDTH + i * WIDTH // PIECES, WIDTH + (i + 1) * WIDTH // PIECES)
            block += dot(attended[:, rows], other_buf[i, :, columns], ((1,), (0,)))
        out_ref[m] = block.astype(jnp.bfloat16)


def mix_kernel(sel_ref, router_ref, hidden_ref, parts_ref, out_ref):
    halves = []
    for half in range(C):
        update = jnp.zeros((HALF, WIDTH), jnp.float32)
        for y in range(Y):
            update += parts_ref[y * C + half].astype(jnp.float32)
        halves.append(update.astype(jnp.bfloat16))
    hot = one_hot(sel_ref[...])
    spread = dot(hot.astype(jnp.bfloat16), jnp.concatenate(halves, axis=0), ((1,), (0,)))
    taken = jnp.max(hot, axis=1, keepdims=True) > 0.0
    eye = lax.broadcasted_iota(jnp.int32, (CAP, CAP), 0) == lax.broadcasted_iota(
        jnp.int32, (CAP, CAP), 1
    )
    for b in range(TOK // CAP):
        rows = slice(b * CAP, (b + 1) * CAP)
        router = jnp.sum(jnp.where(eye, router_ref[:, rows], 0.0), axis=1, keepdims=True)
        before = hidden_ref[rows, :].astype(jnp.float32)
        fresh = before + router * spread[rows]
        out_ref[rows, :] = jnp.where(taken[rows], fresh, before).astype(jnp.bfloat16)


def call(kernel, out_shape, count, scratch=(), smem_first=False, loose=0, flops=0, nbytes=0, vmem=VMEM):
    specs = [in_vmem] * (count - loose) + [in_hbm] * loose
    if smem_first:
        specs[0] = in_smem
    many = isinstance(out_shape, (tuple, list))
    return pl.pallas_call(
        kernel,
        out_shape=out_shape,
        in_specs=specs,
        out_specs=[in_vmem] * len(out_shape) if many else in_vmem,
        scratch_shapes=list(scratch),
        compiler_params=pltpu.CompilerParams(vmem_limit_bytes=vmem),
        cost_estimate=pl.CostEstimate(flops=flops, bytes_accessed=nbytes, transcendentals=0),
    )


def local(
    hidden_state,
    router_weight,
    norm_gain,
    query_weight,
    kv_weight,
    out_weight,
    sel_rows,
    dest_shard,
    dest_slot,
):
    zh, zp, x = lax.axis_index("zh"), lax.axis_index("zp"), lax.axis_index("x")
    y, core = lax.axis_index("y"), lax.axis_index("c")
    is_key = y < Y // 2
    place = jnp.stack([zh, zp, x, core]).astype(jnp.int32)
    core_at = core.astype(jnp.int32)[None]
    sel = sel_rows.reshape(1, CAP)
    swap = [(0, 1), (1, 0)]

    with jax.named_scope("pick"):
        picked = call(pick_kernel, shape((N_MP, HALF, WIDTH)), 2, vmem=WHOLE)(sel, hidden_state)
    with jax.named_scope("gather_features"):
        own_rows = lax.all_to_all(picked, MP, 0, 0, tiled=True)
        deep = WIDTH // PIECES
        out_other = [
            lax.ppermute(out_weight[i * deep : (i + 1) * deep], "c", swap) for i in range(PIECES)
        ]
        own_rows, *out_other = lax.optimization_barrier((own_rows, *out_other))
        other_rows = lax.ppermute(own_rows, "c", swap)

    with jax.named_scope("touch"):
        touched = call(touch_kernel, shape((16, HEAD_DIM)), 2, loose=1)(kv_weight, picked)
    with jax.named_scope("rotation"):
        positions = ((zh * ZP + zp) * X + x) * TOK + jnp.maximum(sel_rows, 0)
        freqs = ROPE_BASE ** (-(jnp.arange(HALF_DIM, dtype=jnp.float32) * 2.0 / HEAD_DIM))
        angles = positions.astype(jnp.float32)[:, None] * freqs[None, :]
        cosine, sine = jnp.cos(angles), jnp.sin(angles)
        cos_q = jnp.concatenate([cosine, cosine], axis=1)
        sin_q = jnp.concatenate([-sine, sine], axis=1)
        cos_kv = jnp.where(is_key, cos_q, 1.0)
        sin_kv = jnp.where(is_key, sin_q, 0.0)
        lane = jnp.arange(HEAD_DIM, dtype=jnp.int32)[None, :]
        mark = jnp.where(is_key & (sel_rows < 0)[:, None] & (lane == 0), UNUSED, 0.0)

    with jax.named_scope("keys_values"):
        normed, kv = call(
            norm_kv_kernel,
            [shape((CAP, N_MP * WIDTH)), shape((CAP, HEAD_DIM))],
            9,
            smem_first=True,
            flops=2 * CAP * 4096 * HEAD_DIM,
            nbytes=3 << 20,
        )(core_at, own_rows, other_rows, norm_gain.reshape(N_MP, WIDTH), cos_kv, sin_kv, mark, kv_weight, touched)
        to_heads = [(m, 2 * m if m < Y else 2 * (m - Y) + 1) for m in range(N_MP)]
        kv = lax.ppermute(kv, MP, to_heads)
    with jax.named_scope("queries"):
        mine, theirs = call(
            query_kernel,
            [shape((HEADS * HALF, HEAD_DIM)), shape((HEADS * HALF, HEAD_DIM))],
            5,
            smem_first=True,
            flops=2 * CAP * N_MP * WIDTH * WIDTH,
            nbytes=3 << 20,
        )(core_at, normed, cos_q, sin_q, query_weight)
        both = jnp.concatenate([mine, theirs], axis=0)
        swapped = lax.ppermute(both, "zp", swap)
        kv, swapped = lax.optimization_barrier((kv, swapped))
    with jax.named_scope("spread_keys_values"):
        kv = jnp.broadcast_to(kv[None], (ZH, CAP, HEAD_DIM))
        kv, both, swapped = lax.optimization_barrier((kv, both, swapped))
        own = lax.all_to_all(kv, "zh", 0, 0, tiled=True)
    with jax.named_scope("share_queries"):
        half = HEADS * HALF
        away = lax.ppermute(jnp.concatenate([both[half:], swapped[half:]], axis=0), "c", swap)
        queries = jnp.concatenate([both[:half], away[:half], swapped[:half], away[half:]], axis=0)
        queries = lax.all_gather(queries, "x", axis=0, tiled=True)
        own, queries = lax.optimization_barrier((own, queries))
        other = lax.ppermute(own, "c", swap)
    with jax.named_scope("attend"):
        columns = GROUP * ROWS
        parts = call(
            attend_kernel,
            shape((GROUP, HEAD_DIM + STATS, ROWS)),
            4,
            scratch=(
                pltpu.VMEM((1, columns), jnp.float32),
                pltpu.VMEM((1, columns), jnp.float32),
                pltpu.VMEM((HEAD_DIM, columns), jnp.float32),
            ),
            smem_first=True,
            flops=4 * columns * HEAD_DIM * ZH * CAP,
            nbytes=2 << 20,
        )(place, queries, own, other)
        parts = lax.all_to_all(parts, NEAR, 0, 0, tiled=True)
    with jax.named_scope("project"):
        partial = call(
            project_kernel,
            shape((N_MP, HALF, WIDTH)),
            2 + PIECES,
            loose=PIECES,
            scratch=(
                pltpu.VMEM((PIECES, WIDTH // PIECES, N_MP * WIDTH), jnp.bfloat16),
                pltpu.VMEM((N_MP, HALF, WIDTH), jnp.float32),
                pltpu.SemaphoreType.DMA((PIECES,)),
            ),
            flops=2 * CAP * WIDTH * N_MP * WIDTH,
            nbytes=5 << 20,
        )(parts, out_weight, *out_other)
        partial = lax.all_to_all(partial, MP, 0, 0, tiled=True)
    with jax.named_scope("mix"):
        return call(mix_kernel, shape((TOK, WIDTH)), 4, nbytes=2 << 20)(
            sel, router_weight.reshape(1, TOK), hidden_state, partial
        )


def solution(mesh):
    fine = Mesh(mesh.devices.reshape(ZH, ZP, X, Y, C), AXES)
    in_specs = (
        P(SEQ, MP),
        P(SEQ),
        P(),
        P(None, MP),
        P(None, MP),
        P(MP, None),
        P(SEQ),
        P(SEQ),
        P(SEQ),
    )
    return jax.shard_map(
        local, mesh=fine, in_specs=in_specs, out_specs=P(SEQ, MP), check_vma=False
    )
```

```python
import functools
import math

import jax
import jax.numpy as jnp
from jax import lax
from jax.experimental import pallas as pl
from jax.experimental.pallas import tpu as pltpu
from jax.sharding import Mesh
from jax.sharding import PartitionSpec as P

HEAD_DIM = 128
HALF_DIM = HEAD_DIM // 2
ROPE_BASE = 500000.0
EPS = 1e-05

ZH, ZP, X, Y, C = 8, 2, 4, 8, 2
AXES = ("zh", "zp", "x", "y", "c")
SEQ, MP = ("zh", "zp", "x"), ("y", "c")
NEAR = ("zp", "x")
GROUP = ZP * X
N_MP = Y * C
CAP = 128
HALF = CAP // C
TOK = 512
WIDTH = 256
HEADS = WIDTH // HEAD_DIM
ROWS = C * HEADS * HALF
STATS = 16
UNUSED = 1e30
PIECES = 4
CHAINS = 1
LOW, LOWER = -1e30, -2e30
VMEM = 48 * 1024 * 1024
WHOLE = 62 * 1024 * 1024

in_vmem = pl.BlockSpec(memory_space=pltpu.VMEM)
in_smem = pl.BlockSpec(memory_space=pltpu.SMEM)
in_hbm = pl.BlockSpec(memory_space=pltpu.HBM)


def shape(dims, dtype=jnp.bfloat16):
    return jax.ShapeDtypeStruct(dims, dtype)


def dot(a, b, contract):
    return lax.dot_general(a, b, (contract, ((), ())), preferred_element_type=jnp.float32)


def one_hot(sel_row):
    rows = lax.broadcasted_iota(jnp.int32, (TOK, CAP), 0)
    return jnp.where(rows == sel_row, 1.0, 0.0)


def turn(head, cosine, sine):
    return head * cosine + pltpu.roll(head, HALF_DIM, 1) * sine


def pick_kernel(sel_ref, hidden_ref, out_ref):
    hot = one_hot(sel_ref[...]).astype(jnp.bfloat16)
    picked = dot(hot, hidden_ref[...], ((0,), (0,))).astype(jnp.bfloat16)
    for m in range(N_MP):
        half = m % C
        out_ref[m] = picked[half * HALF : (half + 1) * HALF]


def touch_kernel(weight_ref, after_ref, out_ref):
    del after_ref
    out_ref[...] = weight_ref[:16, :HEAD_DIM]


def norm_kv_kernel(
    core_ref,
    own_ref,
    other_ref,
    gain_ref,
    cos_ref,
    sin_ref,
    mark_ref,
    weight_ref,
    after_ref,
    normed_ref,
    kv_ref,
):
    del after_ref
    core = core_ref[0]
    for ref, half in ((own_ref, core), (other_ref, 1 - core)):
        square = jnp.zeros((HALF, WIDTH), jnp.float32)
        for m in range(N_MP):
            vals = ref[m].astype(jnp.float32)
            square += vals * vals
        mean = jnp.sum(square, axis=1, keepdims=True) / (N_MP * WIDTH)
        inverse = lax.rsqrt(mean + EPS)
        first = pl.multiple_of(half * HALF, HALF)
        for m in range(N_MP):
            vals = ref[m].astype(jnp.float32) * inverse * gain_ref[m : m + 1, :]
            normed_ref[pl.ds(first, HALF), m * WIDTH : (m + 1) * WIDTH] = vals.astype(jnp.bfloat16)
    total = dot(normed_ref[...], weight_ref[...], ((1,), (0,)))
    kv_ref[...] = (turn(total, cos_ref[...], sin_ref[...]) + mark_ref[...]).astype(jnp.bfloat16)


def lay_kernel(kv_ref, out_ref):
    for t in range(ZH):
        out_ref[t] = kv_ref[...]


def query_kernel(core_ref, normed_ref, cos_ref, sin_ref, weight_ref, mine_ref, theirs_ref):
    core = core_ref[0]
    total = dot(normed_ref[...], weight_ref[...], ((1,), (0,)))
    for h in range(HEADS):
        head = total[:, h * HEAD_DIM : (h + 1) * HEAD_DIM]
        turned = turn(head, cos_ref[...], sin_ref[...]).astype(jnp.bfloat16)
        lower, upper = turned[:HALF], turned[HALF:]
        rows = slice(h * HALF, (h + 1) * HALF)
        mine_ref[rows, :] = jnp.where(core == 0, lower, upper)
        theirs_ref[rows, :] = jnp.where(core == 0, upper, lower)


def attend_kernel(place_ref, query_ref, own_ref, other_ref, out_ref, high_ref, sum_ref, acc_ref):
    zh, zp, x, c = place_ref[0], place_ref[1], place_ref[2], place_ref[3]
    columns = GROUP * ROWS
    scale = math.log2(math.e) / math.sqrt(HEAD_DIM)
    high_ref[...] = jnp.full(high_ref.shape, LOW, jnp.float32)
    sum_ref[...] = jnp.zeros(sum_ref.shape, jnp.float32)
    acc_ref[...] = jnp.zeros(acc_ref.shape, jnp.float32)
    column = lax.broadcasted_iota(jnp.int32, (1, columns), 1)
    swapped = column // ROWS % ZP
    query_zp = zp + swapped - 2 * zp * swapped
    query_shard = (zh * ZP + query_zp) * X + column // (ZP * ROWS)
    query_order = query_shard * CAP + c * HALF + column % HALF

    def step(pair, carry):
        own = own_ref[pl.ds(2 * pair, 2)].reshape(2 * CAP, HEAD_DIM)
        other = other_ref[pl.ds(2 * pair, 2)].reshape(2 * CAP, HEAD_DIM)
        keys = jnp.where(c == 0, own, other)
        values_t = jnp.where(c == 0, other, own).T
        row = lax.broadcasted_iota(jnp.int32, (2 * CAP, 1), 0)
        shard = ((2 * pair + row // CAP) * ZP + zp) * X + x
        key_order = shard * CAP + row % CAP
        unused = keys[:, 0:1].astype(jnp.float32) > 0.1 * UNUSED
        key_order = jnp.where(unused, 1 << 30, key_order)
        for part in range(CHAINS):
            span = slice(part * columns // CHAINS, (part + 1) * columns // CHAINS)
            scores = dot(keys, query_ref[span, :], ((1,), (1,))) * scale
            scores = jnp.where(key_order <= query_order[:, span], scores, LOWER)
            before = high_ref[:, span]
            high = jnp.maximum(before, jnp.max(scores, axis=0, keepdims=True))
            weights = jnp.exp2(scores - high)
            fade = jnp.exp2(before - high)
            high_ref[:, span] = high
            sum_ref[:, span] = sum_ref[:, span] * fade + jnp.sum(weights, axis=0, keepdims=True)
            acc_ref[:, span] = acc_ref[:, span] * fade + dot(
                values_t, weights.astype(jnp.bfloat16), ((1,), (0,))
            )
        return carry

    lax.fori_loop(0, zh // 2 + 1, step, 0)
    total = sum_ref[...]
    safe = jnp.maximum(total, 1e-30)
    attended = (acc_ref[...] / safe).astype(jnp.bfloat16)
    stat_row = lax.broadcasted_iota(jnp.int32, (STATS, columns), 0)
    stats = jnp.zeros((STATS, columns), jnp.float32)
    left = jnp.where(total > 0.0, high_ref[...] + jnp.log2(safe), LOW)
    for k in range(3):
        piece = left.astype(jnp.bfloat16).astype(jnp.float32)
        stats = jnp.where(stat_row == k, piece, stats)
        left = left - piece
    stats = stats.astype(jnp.bfloat16)
    for to_x in range(X):
        for swap in range(ZP):
            first = (to_x * ZP + swap) * ROWS
            home = (zp + swap - 2 * zp * swap) * X + to_x
            out_ref[home, :HEAD_DIM, :] = attended[:, first : first + ROWS]
            out_ref[home, HEAD_DIM:, :] = stats[:, first : first + ROWS]


def project_kernel(parts_ref, own_ref, *refs):
    other_refs, (out_ref, other_buf, total_ref, arrived) = refs[:PIECES], refs[PIECES:]
    copies = [
        pltpu.make_async_copy(ref, other_buf.at[i], arrived.at[i])
        for i, ref in enumerate(other_refs)
    ]
    for copy in copies:
        copy.start()
    logs = []
    for t in range(GROUP):
        stats = parts_ref[t, HEAD_DIM:, :].astype(jnp.float32)
        logs.append(stats[0:1] + stats[1:2] + stats[2:3])
    high = functools.reduce(jnp.maximum, logs)
    shares = [jnp.exp2(v - high) for v in logs]
    total = functools.reduce(jnp.add, shares)
    merged = jnp.zeros((HEAD_DIM, ROWS), jnp.float32)
    for t in range(GROUP):
        part = parts_ref[t, :HEAD_DIM, :].astype(jnp.float32)
        merged += part * (shares[t] / total)
    merged = merged.T.astype(jnp.bfloat16)
    attended = jnp.concatenate(
        [merged[j * HALF : (j + 1) * HALF] for j in range(C * HEADS)], axis=1
    )
    for m in range(N_MP):
        columns = slice(m * WIDTH, (m + 1) * WIDTH)
        total_ref[m] = dot(attended[:, :WIDTH], own_ref[:, columns], ((1,), (0,)))
    for copy in copies:
        copy.wait()
    for m in range(N_MP):
        columns = slice(m * WIDTH, (m + 1) * WIDTH)
        block = total_ref[m]
        for i in range(PIECES):
            rows = slice(WIDTH + i * WIDTH // PIECES, WIDTH + (i + 1) * WIDTH // PIECES)
            block += dot(attended[:, rows], other_buf[i, :, columns], ((1,), (0,)))
        out_ref[m] = block.astype(jnp.bfloat16)


def mix_kernel(sel_ref, router_ref, hidden_ref, parts_ref, out_ref):
    halves = []
    for half in range(C):
        update = jnp.zeros((HALF, WIDTH), jnp.float32)
        for y in range(Y):
            update += parts_ref[y * C + half].astype(jnp.float32)
        halves.append(update.astype(jnp.bfloat16))
    hot = one_hot(sel_ref[...])
    spread = dot(hot.astype(jnp.bfloat16), jnp.concatenate(halves, axis=0), ((1,), (0,)))
    taken = jnp.max(hot, axis=1, keepdims=True) > 0.0
    eye = lax.broadcasted_iota(jnp.int32, (CAP, CAP), 0) == lax.broadcasted_iota(
        jnp.int32, (CAP, CAP), 1
    )
    for b in range(TOK // CAP):
        rows = slice(b * CAP, (b + 1) * CAP)
        router = jnp.sum(jnp.where(eye, router_ref[:, rows], 0.0), axis=1, keepdims=True)
        before = hidden_ref[rows, :].astype(jnp.float32)
        fresh = before + router * spread[rows]
        out_ref[rows, :] = jnp.where(taken[rows], fresh, before).astype(jnp.bfloat16)


def call(kernel, out_shape, count, scratch=(), smem_first=False, loose=0, flops=0, nbytes=0, vmem=VMEM):
    specs = [in_vmem] * (count - loose) + [in_hbm] * loose
    if smem_first:
        specs[0] = in_smem
    many = isinstance(out_shape, (tuple, list))
    return pl.pallas_call(
        kernel,
        out_shape=out_shape,
        in_specs=specs,
        out_specs=[in_vmem] * len(out_shape) if many else in_vmem,
        scratch_shapes=list(scratch),
        compiler_params=pltpu.CompilerParams(vmem_limit_bytes=vmem),
        cost_estimate=pl.CostEstimate(flops=flops, bytes_accessed=nbytes, transcendentals=0),
    )


def local(
    hidden_state,
    router_weight,
    norm_gain,
    query_weight,
    kv_weight,
    out_weight,
    sel_rows,
    dest_shard,
    dest_slot,
):
    zh, zp, x = lax.axis_index("zh"), lax.axis_index("zp"), lax.axis_index("x")
    y, core = lax.axis_index("y"), lax.axis_index("c")
    is_key = y < Y // 2
    place = jnp.stack([zh, zp, x, core]).astype(jnp.int32)
    core_at = core.astype(jnp.int32)[None]
    sel = sel_rows.reshape(1, CAP)
    swap = [(0, 1), (1, 0)]

    with jax.named_scope("pick"):
        picked = call(pick_kernel, shape((N_MP, HALF, WIDTH)), 2, vmem=WHOLE)(sel, hidden_state)
    with jax.named_scope("gather_features"):
        own_rows = lax.all_to_all(picked, MP, 0, 0, tiled=True)
        deep = WIDTH // PIECES
        out_other = [
            lax.ppermute(out_weight[i * deep : (i + 1) * deep], "c", swap) for i in range(PIECES)
        ]
        own_rows, *out_other = lax.optimization_barrier((own_rows, *out_other))
        other_rows = lax.ppermute(own_rows, "c", swap)

    with jax.named_scope("touch"):
        touched = call(touch_kernel, shape((16, HEAD_DIM)), 2, loose=1)(kv_weight, picked)
    with jax.named_scope("rotation"):
        positions = ((zh * ZP + zp) * X + x) * TOK + jnp.maximum(sel_rows, 0)
        freqs = ROPE_BASE ** (-(jnp.arange(HALF_DIM, dtype=jnp.float32) * 2.0 / HEAD_DIM))
        angles = positions.astype(jnp.float32)[:, None] * freqs[None, :]
        cosine, sine = jnp.cos(angles), jnp.sin(angles)
        cos_q = jnp.concatenate([cosine, cosine], axis=1)
        sin_q = jnp.concatenate([-sine, sine], axis=1)
        cos_kv = jnp.where(is_key, cos_q, 1.0)
        sin_kv = jnp.where(is_key, sin_q, 0.0)
        lane = jnp.arange(HEAD_DIM, dtype=jnp.int32)[None, :]
        mark = jnp.where(is_key & (sel_rows < 0)[:, None] & (lane == 0), UNUSED, 0.0)

    with jax.named_scope("keys_values"):
        normed, kv = call(
            norm_kv_kernel,
            [shape((CAP, N_MP * WIDTH)), shape((CAP, HEAD_DIM))],
            9,
            smem_first=True,
            flops=2 * CAP * 4096 * HEAD_DIM,
            nbytes=3 << 20,
        )(core_at, own_rows, other_rows, norm_gain.reshape(N_MP, WIDTH), cos_kv, sin_kv, mark, kv_weight, touched)
        to_heads = [(m, 2 * m if m < Y else 2 * (m - Y) + 1) for m in range(N_MP)]
        kv = lax.ppermute(kv, MP, to_heads)
        kv = call(lay_kernel, shape((ZH, CAP, HEAD_DIM)), 1, flops=1 << 35, nbytes=64 << 20)(kv)
    with jax.named_scope("queries"):
        mine, theirs = call(
            query_kernel,
            [shape((HEADS * HALF, HEAD_DIM)), shape((HEADS * HALF, HEAD_DIM))],
            5,
            smem_first=True,
            flops=2 * CAP * N_MP * WIDTH * WIDTH,
            nbytes=3 << 20,
        )(core_at, normed, cos_q, sin_q, query_weight)
        both = jnp.concatenate([mine, theirs], axis=0)
        swapped = lax.ppermute(both, "zp", swap)
        kv, both = lax.optimization_barrier((kv, both))
    with jax.named_scope("spread_keys_values"):
        own = lax.all_to_all(kv, "zh", 0, 0, tiled=True)
    with jax.named_scope("share_queries"):
        half = HEADS * HALF
        away = lax.ppermute(jnp.concatenate([both[half:], swapped[half:]], axis=0), "c", swap)
        queries = jnp.concatenate([both[:half], away[:half], swapped[:half], away[half:]], axis=0)
        queries = lax.all_gather(queries, "x", axis=0, tiled=True)
        own, queries = lax.optimization_barrier((own, queries))
        other = lax.ppermute(own, "c", swap)
    with jax.named_scope("attend"):
        columns = GROUP * ROWS
        parts = call(
            attend_kernel,
            shape((GROUP, HEAD_DIM + STATS, ROWS)),
            4,
            scratch=(
                pltpu.VMEM((1, columns), jnp.float32),
                pltpu.VMEM((1, columns), jnp.float32),
                pltpu.VMEM((HEAD_DIM, columns), jnp.float32),
            ),
            smem_first=True,
            flops=4 * columns * HEAD_DIM * ZH * CAP,
            nbytes=2 << 20,
        )(place, queries, own, other)
        parts = lax.all_to_all(parts, NEAR, 0, 0, tiled=True)
    with jax.named_scope("project"):
        partial = call(
            project_kernel,
            shape((N_MP, HALF, WIDTH)),
            2 + PIECES,
            loose=PIECES,
            scratch=(
                pltpu.VMEM((PIECES, WIDTH // PIECES, N_MP * WIDTH), jnp.bfloat16),
                pltpu.VMEM((N_MP, HALF, WIDTH), jnp.float32),
                pltpu.SemaphoreType.DMA((PIECES,)),
            ),
            flops=2 * CAP * WIDTH * N_MP * WIDTH,
            nbytes=5 << 20,
        )(parts, out_weight, *out_other)
        partial = lax.all_to_all(partial, MP, 0, 0, tiled=True)
    with jax.named_scope("mix"):
        return call(mix_kernel, shape((TOK, WIDTH)), 4, nbytes=2 << 20)(
            sel, router_weight.reshape(1, TOK), hidden_state, partial
        )


def solution(mesh):
    fine = Mesh(mesh.devices.reshape(ZH, ZP, X, Y, C), AXES)
    in_specs = (
        P(SEQ, MP),
        P(SEQ),
        P(),
        P(None, MP),
        P(None, MP),
        P(MP, None),
        P(SEQ),
        P(SEQ),
        P(SEQ),
    )
    return jax.shard_map(
        local, mesh=fine, in_specs=in_specs, out_specs=P(SEQ, MP), check_vma=False
    )
```

```python
import functools
import math

import jax
import jax.numpy as jnp
from jax import lax
from jax.experimental import pallas as pl
from jax.experimental.pallas import tpu as pltpu
from jax.sharding import Mesh
from jax.sharding import PartitionSpec as P

HEAD_DIM = 128
HALF_DIM = HEAD_DIM // 2
ROPE_BASE = 500000.0
EPS = 1e-05

ZH, ZP, X, Y, C = 8, 2, 4, 8, 2
AXES = ("zh", "zp", "x", "y", "c")
SEQ, MP = ("zh", "zp", "x"), ("y", "c")
NEAR = ("zp", "x")
GROUP = ZP * X
N_MP = Y * C
CAP = 128
HALF = CAP // C
TOK = 512
WIDTH = 256
HEADS = WIDTH // HEAD_DIM
ROWS = C * HEADS * HALF
STATS = 16
UNUSED = 1e30
PIECES = 4
CHAINS = 1
LOW, LOWER = -1e30, -2e30
VMEM = 48 * 1024 * 1024
WHOLE = 62 * 1024 * 1024

in_vmem = pl.BlockSpec(memory_space=pltpu.VMEM)
in_smem = pl.BlockSpec(memory_space=pltpu.SMEM)
in_hbm = pl.BlockSpec(memory_space=pltpu.HBM)


def shape(dims, dtype=jnp.bfloat16):
    return jax.ShapeDtypeStruct(dims, dtype)


def dot(a, b, contract):
    return lax.dot_general(a, b, (contract, ((), ())), preferred_element_type=jnp.float32)


def one_hot(sel_row):
    rows = lax.broadcasted_iota(jnp.int32, (TOK, CAP), 0)
    return jnp.where(rows == sel_row, 1.0, 0.0)


def turn(head, cosine, sine):
    return head * cosine + pltpu.roll(head, HALF_DIM, 1) * sine


def pick_kernel(sel_ref, hidden_ref, out_ref):
    hot = one_hot(sel_ref[...]).astype(jnp.bfloat16)
    picked = dot(hot, hidden_ref[...], ((0,), (0,))).astype(jnp.bfloat16)
    for m in range(N_MP):
        half = m % C
        out_ref[m] = picked[half * HALF : (half + 1) * HALF]


def touch_kernel(weight_ref, after_ref, out_ref):
    del after_ref
    out_ref[...] = weight_ref[:16, :HEAD_DIM]


def norm_kv_kernel(
    core_ref,
    own_ref,
    other_ref,
    gain_ref,
    cos_ref,
    sin_ref,
    mark_ref,
    weight_ref,
    after_ref,
    normed_ref,
    kv_ref,
):
    del after_ref
    core = core_ref[0]
    for ref, half in ((own_ref, core), (other_ref, 1 - core)):
        square = jnp.zeros((HALF, WIDTH), jnp.float32)
        for m in range(N_MP):
            vals = ref[m].astype(jnp.float32)
            square += vals * vals
        mean = jnp.sum(square, axis=1, keepdims=True) / (N_MP * WIDTH)
        inverse = lax.rsqrt(mean + EPS)
        first = pl.multiple_of(half * HALF, HALF)
        for m in range(N_MP):
            vals = ref[m].astype(jnp.float32) * inverse * gain_ref[m : m + 1, :]
            normed_ref[pl.ds(first, HALF), m * WIDTH : (m + 1) * WIDTH] = vals.astype(jnp.bfloat16)
    total = dot(normed_ref[...], weight_ref[...], ((1,), (0,)))
    kv_ref[...] = (turn(total, cos_ref[...], sin_ref[...]) + mark_ref[...]).astype(jnp.bfloat16)


def lay_kernel(kv_ref, out_ref):
    for t in range(ZH):
        out_ref[t] = kv_ref[...]


def query_kernel(core_ref, normed_ref, cos_ref, sin_ref, weight_ref, mine_ref, theirs_ref):
    core = core_ref[0]
    total = dot(normed_ref[...], weight_ref[...], ((1,), (0,)))
    for h in range(HEADS):
        head = total[:, h * HEAD_DIM : (h + 1) * HEAD_DIM]
        turned = turn(head, cos_ref[...], sin_ref[...]).astype(jnp.bfloat16)
        lower, upper = turned[:HALF], turned[HALF:]
        rows = slice(h * HALF, (h + 1) * HALF)
        mine_ref[rows, :] = jnp.where(core == 0, lower, upper)
        theirs_ref[rows, :] = jnp.where(core == 0, upper, lower)


def attend_kernel(place_ref, query_ref, own_ref, other_ref, out_ref, high_ref, sum_ref, acc_ref):
    zh, zp, x, c = place_ref[0], place_ref[1], place_ref[2], place_ref[3]
    columns = GROUP * ROWS
    scale = math.log2(math.e) / math.sqrt(HEAD_DIM)
    high_ref[...] = jnp.full(high_ref.shape, LOW, jnp.float32)
    sum_ref[...] = jnp.zeros(sum_ref.shape, jnp.float32)
    acc_ref[...] = jnp.zeros(acc_ref.shape, jnp.float32)
    column = lax.broadcasted_iota(jnp.int32, (1, columns), 1)
    swapped = column // ROWS % ZP
    query_zp = zp + swapped - 2 * zp * swapped
    query_shard = (zh * ZP + query_zp) * X + column // (ZP * ROWS)
    query_order = query_shard * CAP + c * HALF + column % HALF

    def step(pair, carry):
        own = own_ref[pl.ds(2 * pair, 2)].reshape(2 * CAP, HEAD_DIM)
        other = other_ref[pl.ds(2 * pair, 2)].reshape(2 * CAP, HEAD_DIM)
        keys = jnp.where(c == 0, own, other)
        values_t = jnp.where(c == 0, other, own).T
        row = lax.broadcasted_iota(jnp.int32, (2 * CAP, 1), 0)
        shard = ((2 * pair + row // CAP) * ZP + zp) * X + x
        key_order = shard * CAP + row % CAP
        unused = keys[:, 0:1].astype(jnp.float32) > 0.1 * UNUSED
        key_order = jnp.where(unused, 1 << 30, key_order)
        for part in range(CHAINS):
            span = slice(part * columns // CHAINS, (part + 1) * columns // CHAINS)
            scores = dot(keys, query_ref[span, :], ((1,), (1,))) * scale
            scores = jnp.where(key_order <= query_order[:, span], scores, LOWER)
            before = high_ref[:, span]
            high = jnp.maximum(before, jnp.max(scores, axis=0, keepdims=True))
            weights = jnp.exp2(scores - high)
            fade = jnp.exp2(before - high)
            high_ref[:, span] = high
            sum_ref[:, span] = sum_ref[:, span] * fade + jnp.sum(weights, axis=0, keepdims=True)
            acc_ref[:, span] = acc_ref[:, span] * fade + dot(
                values_t, weights.astype(jnp.bfloat16), ((1,), (0,))
            )
        return carry

    lax.fori_loop(0, zh // 2 + 1, step, 0)
    total = sum_ref[...]
    safe = jnp.maximum(total, 1e-30)
    attended = (acc_ref[...] / safe).astype(jnp.bfloat16)
    stat_row = lax.broadcasted_iota(jnp.int32, (STATS, columns), 0)
    stats = jnp.zeros((STATS, columns), jnp.float32)
    left = jnp.where(total > 0.0, high_ref[...] + jnp.log2(safe), LOW)
    for k in range(3):
        piece = left.astype(jnp.bfloat16).astype(jnp.float32)
        stats = jnp.where(stat_row == k, piece, stats)
        left = left - piece
    stats = stats.astype(jnp.bfloat16)
    for to_x in range(X):
        for swap in range(ZP):
            first = (to_x * ZP + swap) * ROWS
            home = (zp + swap - 2 * zp * swap) * X + to_x
            out_ref[home, :HEAD_DIM, :] = attended[:, first : first + ROWS]
            out_ref[home, HEAD_DIM:, :] = stats[:, first : first + ROWS]


def project_kernel(parts_ref, own_ref, *refs):
    other_refs, (out_ref, other_buf, total_ref, arrived) = refs[:PIECES], refs[PIECES:]
    copies = [
        pltpu.make_async_copy(ref, other_buf.at[i], arrived.at[i])
        for i, ref in enumerate(other_refs)
    ]
    for copy in copies:
        copy.start()
    logs = []
    for t in range(GROUP):
        stats = parts_ref[t, HEAD_DIM:, :].astype(jnp.float32)
        logs.append(stats[0:1] + stats[1:2] + stats[2:3])
    high = functools.reduce(jnp.maximum, logs)
    shares = [jnp.exp2(v - high) for v in logs]
    total = functools.reduce(jnp.add, shares)
    merged = jnp.zeros((HEAD_DIM, ROWS), jnp.float32)
    for t in range(GROUP):
        part = parts_ref[t, :HEAD_DIM, :].astype(jnp.float32)
        merged += part * (shares[t] / total)
    merged = merged.T.astype(jnp.bfloat16)
    attended = jnp.concatenate(
        [merged[j * HALF : (j + 1) * HALF] for j in range(C * HEADS)], axis=1
    )
    for m in range(N_MP):
        columns = slice(m * WIDTH, (m + 1) * WIDTH)
        total_ref[m] = dot(attended[:, :WIDTH], own_ref[:, columns], ((1,), (0,)))
    for copy in copies:
        copy.wait()
    for m in range(N_MP):
        columns = slice(m * WIDTH, (m + 1) * WIDTH)
        block = total_ref[m]
        for i in range(PIECES):
            rows = slice(WIDTH + i * WIDTH // PIECES, WIDTH + (i + 1) * WIDTH // PIECES)
            block += dot(attended[:, rows], other_buf[i, :, columns], ((1,), (0,)))
        out_ref[m] = block.astype(jnp.bfloat16)


def mix_kernel(sel_ref, router_ref, hidden_ref, parts_ref, out_ref):
    halves = []
    for half in range(C):
        update = jnp.zeros((HALF, WIDTH), jnp.float32)
        for y in range(Y):
            update += parts_ref[y * C + half].astype(jnp.float32)
        halves.append(update.astype(jnp.bfloat16))
    hot = one_hot(sel_ref[...])
    spread = dot(hot.astype(jnp.bfloat16), jnp.concatenate(halves, axis=0), ((1,), (0,)))
    taken = jnp.max(hot, axis=1, keepdims=True) > 0.0
    eye = lax.broadcasted_iota(jnp.int32, (CAP, CAP), 0) == lax.broadcasted_iota(
        jnp.int32, (CAP, CAP), 1
    )
    for b in range(TOK // CAP):
        rows = slice(b * CAP, (b + 1) * CAP)
        router = jnp.sum(jnp.where(eye, router_ref[:, rows], 0.0), axis=1, keepdims=True)
        before = hidden_ref[rows, :].astype(jnp.float32)
        fresh = before + router * spread[rows]
        out_ref[rows, :] = jnp.where(taken[rows], fresh, before).astype(jnp.bfloat16)


def call(kernel, out_shape, count, scratch=(), smem_first=False, loose=0, flops=0, nbytes=0, vmem=VMEM):
    specs = [in_vmem] * (count - loose) + [in_hbm] * loose
    if smem_first:
        specs[0] = in_smem
    many = isinstance(out_shape, (tuple, list))
    return pl.pallas_call(
        kernel,
        out_shape=out_shape,
        in_specs=specs,
        out_specs=[in_vmem] * len(out_shape) if many else in_vmem,
        scratch_shapes=list(scratch),
        compiler_params=pltpu.CompilerParams(vmem_limit_bytes=vmem),
        cost_estimate=pl.CostEstimate(flops=flops, bytes_accessed=nbytes, transcendentals=0),
    )


def local(
    hidden_state,
    router_weight,
    norm_gain,
    query_weight,
    kv_weight,
    out_weight,
    sel_rows,
    dest_shard,
    dest_slot,
):
    zh, zp, x = lax.axis_index("zh"), lax.axis_index("zp"), lax.axis_index("x")
    y, core = lax.axis_index("y"), lax.axis_index("c")
    is_key = y < Y // 2
    place = jnp.stack([zh, zp, x, core]).astype(jnp.int32)
    core_at = core.astype(jnp.int32)[None]
    sel = sel_rows.reshape(1, CAP)
    swap = [(0, 1), (1, 0)]

    with jax.named_scope("pick"):
        picked = call(pick_kernel, shape((N_MP, HALF, WIDTH)), 2, vmem=WHOLE)(sel, hidden_state)
    with jax.named_scope("gather_features"):
        own_rows = lax.all_to_all(picked, MP, 0, 0, tiled=True)
        deep = WIDTH // PIECES
        out_other = [
            lax.ppermute(out_weight[i * deep : (i + 1) * deep], "c", swap) for i in range(PIECES)
        ]
        own_rows, *out_other = lax.optimization_barrier((own_rows, *out_other))
        other_rows = lax.ppermute(own_rows, "c", swap)

    with jax.named_scope("touch"):
        touched = call(touch_kernel, shape((16, HEAD_DIM)), 2, loose=1)(kv_weight, picked)
    with jax.named_scope("rotation"):
        positions = ((zh * ZP + zp) * X + x) * TOK + jnp.maximum(sel_rows, 0)
        freqs = ROPE_BASE ** (-(jnp.arange(HALF_DIM, dtype=jnp.float32) * 2.0 / HEAD_DIM))
        angles = positions.astype(jnp.float32)[:, None] * freqs[None, :]
        cosine, sine = jnp.cos(angles), jnp.sin(angles)
        cos_q = jnp.concatenate([cosine, cosine], axis=1)
        sin_q = jnp.concatenate([-sine, sine], axis=1)
        cos_kv = jnp.where(is_key, cos_q, 1.0)
        sin_kv = jnp.where(is_key, sin_q, 0.0)
        lane = jnp.arange(HEAD_DIM, dtype=jnp.int32)[None, :]
        mark = jnp.where(is_key & (sel_rows < 0)[:, None] & (lane == 0), UNUSED, 0.0)

    with jax.named_scope("keys_values"):
        normed, kv = call(
            norm_kv_kernel,
            [shape((CAP, N_MP * WIDTH)), shape((CAP, HEAD_DIM))],
            9,
            smem_first=True,
            flops=2 * CAP * 4096 * HEAD_DIM,
            nbytes=3 << 20,
        )(core_at, own_rows, other_rows, norm_gain.reshape(N_MP, WIDTH), cos_kv, sin_kv, mark, kv_weight, touched)
        to_heads = [(m, 2 * m if m < Y else 2 * (m - Y) + 1) for m in range(N_MP)]
        kv = lax.ppermute(kv, MP, to_heads)
        kv = call(lay_kernel, shape((ZH, CAP, HEAD_DIM)), 1, flops=1 << 35, nbytes=64 << 20)(kv)
    with jax.named_scope("queries"):
        mine, theirs = call(
            query_kernel,
            [shape((HEADS * HALF, HEAD_DIM)), shape((HEADS * HALF, HEAD_DIM))],
            5,
            smem_first=True,
            flops=2 * CAP * N_MP * WIDTH * WIDTH,
            nbytes=3 << 20,
        )(core_at, normed, cos_q, sin_q, query_weight)
        both = jnp.concatenate([mine, theirs], axis=0)
        swapped = lax.ppermute(both, "zp", swap)
    with jax.named_scope("spread_keys_values"):
        own = lax.all_to_all(kv, "zh", 0, 0, tiled=True)
    with jax.named_scope("share_queries"):
        half = HEADS * HALF
        away = lax.ppermute(jnp.concatenate([both[half:], swapped[half:]], axis=0), "c", swap)
        queries = jnp.concatenate([both[:half], away[:half], swapped[:half], away[half:]], axis=0)
        queries = lax.all_gather(queries, "x", axis=0, tiled=True)
        own, queries = lax.optimization_barrier((own, queries))
        other = lax.ppermute(own, "c", swap)
    with jax.named_scope("attend"):
        columns = GROUP * ROWS
        parts = call(
            attend_kernel,
            shape((GROUP, HEAD_DIM + STATS, ROWS)),
            4,
            scratch=(
                pltpu.VMEM((1, columns), jnp.float32),
                pltpu.VMEM((1, columns), jnp.float32),
                pltpu.VMEM((HEAD_DIM, columns), jnp.float32),
            ),
            smem_first=True,
            flops=4 * columns * HEAD_DIM * ZH * CAP,
            nbytes=2 << 20,
        )(place, queries, own, other)
        parts = lax.all_to_all(parts, NEAR, 0, 0, tiled=True)
    with jax.named_scope("project"):
        partial = call(
            project_kernel,
            shape((N_MP, HALF, WIDTH)),
            2 + PIECES,
            loose=PIECES,
            scratch=(
                pltpu.VMEM((PIECES, WIDTH // PIECES, N_MP * WIDTH), jnp.bfloat16),
                pltpu.VMEM((N_MP, HALF, WIDTH), jnp.float32),
                pltpu.SemaphoreType.DMA((PIECES,)),
            ),
            flops=2 * CAP * WIDTH * N_MP * WIDTH,
            nbytes=5 << 20,
        )(parts, out_weight, *out_other)
        partial = lax.all_to_all(partial, MP, 0, 0, tiled=True)
    with jax.named_scope("mix"):
        return call(mix_kernel, shape((TOK, WIDTH)), 4, nbytes=2 << 20)(
            sel, router_weight.reshape(1, TOK), hidden_state, partial
        )


def solution(mesh):
    fine = Mesh(mesh.devices.reshape(ZH, ZP, X, Y, C), AXES)
    in_specs = (
        P(SEQ, MP),
        P(SEQ),
        P(),
        P(None, MP),
        P(None, MP),
        P(MP, None),
        P(SEQ),
        P(SEQ),
        P(SEQ),
    )
    return jax.shard_map(
        local, mesh=fine, in_specs=in_specs, out_specs=P(SEQ, MP), check_vma=False
    )
```

```python
import functools
import math

import jax
import jax.numpy as jnp
from jax import lax
from jax.experimental import pallas as pl
from jax.experimental.pallas import tpu as pltpu
from jax.sharding import Mesh
from jax.sharding import PartitionSpec as P

HEAD_DIM = 128
HALF_DIM = HEAD_DIM // 2
ROPE_BASE = 500000.0
EPS = 1e-05

ZH, ZP, X, Y, C = 8, 2, 4, 8, 2
AXES = ("zh", "zp", "x", "y", "c")
SEQ, MP = ("zh", "zp", "x"), ("y", "c")
NEAR = ("zp", "x")
GROUP = ZP * X
N_MP = Y * C
CAP = 128
HALF = CAP // C
TOK = 512
WIDTH = 256
HEADS = WIDTH // HEAD_DIM
ROWS = C * HEADS * HALF
STATS = 16
UNUSED = 1e30
PIECES = 4
CHAINS = 1
LOW, LOWER = -1e30, -2e30
VMEM = 48 * 1024 * 1024
WHOLE = 62 * 1024 * 1024

in_vmem = pl.BlockSpec(memory_space=pltpu.VMEM)
in_smem = pl.BlockSpec(memory_space=pltpu.SMEM)
in_hbm = pl.BlockSpec(memory_space=pltpu.HBM)


def shape(dims, dtype=jnp.bfloat16):
    return jax.ShapeDtypeStruct(dims, dtype)


def dot(a, b, contract):
    return lax.dot_general(a, b, (contract, ((), ())), preferred_element_type=jnp.float32)


def one_hot(sel_row):
    rows = lax.broadcasted_iota(jnp.int32, (TOK, CAP), 0)
    return jnp.where(rows == sel_row, 1.0, 0.0)


def turn(head, cosine, sine):
    return head * cosine + pltpu.roll(head, HALF_DIM, 1) * sine


def pick_kernel(sel_ref, hidden_ref, out_ref):
    hot = one_hot(sel_ref[...]).astype(jnp.bfloat16)
    picked = dot(hot, hidden_ref[...], ((0,), (0,))).astype(jnp.bfloat16)
    for m in range(N_MP):
        half = m % C
        out_ref[m] = picked[half * HALF : (half + 1) * HALF]


def touch_kernel(weight_ref, after_ref, out_ref):
    del after_ref
    out_ref[...] = weight_ref[:16, :HEAD_DIM]


def norm_kv_kernel(
    core_ref,
    own_ref,
    other_ref,
    gain_ref,
    cos_ref,
    sin_ref,
    mark_ref,
    weight_ref,
    after_ref,
    normed_ref,
    kv_ref,
):
    del after_ref
    core = core_ref[0]
    for ref, half in ((own_ref, core), (other_ref, 1 - core)):
        square = jnp.zeros((HALF, WIDTH), jnp.float32)
        for m in range(N_MP):
            vals = ref[m].astype(jnp.float32)
            square += vals * vals
        mean = jnp.sum(square, axis=1, keepdims=True) / (N_MP * WIDTH)
        inverse = lax.rsqrt(mean + EPS)
        first = pl.multiple_of(half * HALF, HALF)
        for m in range(N_MP):
            vals = ref[m].astype(jnp.float32) * inverse * gain_ref[m : m + 1, :]
            normed_ref[pl.ds(first, HALF), m * WIDTH : (m + 1) * WIDTH] = vals.astype(jnp.bfloat16)
    total = dot(normed_ref[...], weight_ref[...], ((1,), (0,)))
    kv_ref[...] = (turn(total, cos_ref[...], sin_ref[...]) + mark_ref[...]).astype(jnp.bfloat16)


def lay_kernel(kv_ref, out_ref):
    for t in range(ZH):
        out_ref[t] = kv_ref[...]


def query_kernel(core_ref, normed_ref, cos_ref, sin_ref, weight_ref, mine_ref, theirs_ref):
    core = core_ref[0]
    total = dot(normed_ref[...], weight_ref[...], ((1,), (0,)))
    for h in range(HEADS):
        head = total[:, h * HEAD_DIM : (h + 1) * HEAD_DIM]
        turned = turn(head, cos_ref[...], sin_ref[...]).astype(jnp.bfloat16)
        lower, upper = turned[:HALF], turned[HALF:]
        rows = slice(h * HALF, (h + 1) * HALF)
        mine_ref[rows, :] = jnp.where(core == 0, lower, upper)
        theirs_ref[rows, :] = jnp.where(core == 0, upper, lower)


def attend_kernel(place_ref, query_ref, own_ref, other_ref, out_ref, high_ref, sum_ref, acc_ref):
    zh, zp, x, c = place_ref[0], place_ref[1], place_ref[2], place_ref[3]
    columns = GROUP * ROWS
    scale = math.log2(math.e) / math.sqrt(HEAD_DIM)
    high_ref[...] = jnp.full(high_ref.shape, LOW, jnp.float32)
    sum_ref[...] = jnp.zeros(sum_ref.shape, jnp.float32)
    acc_ref[...] = jnp.zeros(acc_ref.shape, jnp.float32)
    column = lax.broadcasted_iota(jnp.int32, (1, columns), 1)
    swapped = column // ROWS % ZP
    query_zp = zp + swapped - 2 * zp * swapped
    query_shard = (zh * ZP + query_zp) * X + column // (ZP * ROWS)
    query_order = query_shard * CAP + c * HALF + column % HALF

    def step(far, carry):
        own, other = own_ref[far], other_ref[far]
        keys = jnp.where(c == 0, own, other)
        values_t = jnp.where(c == 0, other, own).T
        entry = lax.broadcasted_iota(jnp.int32, (CAP, 1), 0)
        key_order = ((far * ZP + zp) * X + x) * CAP + entry
        unused = keys[:, 0:1].astype(jnp.float32) > 0.1 * UNUSED
        key_order = jnp.where(unused, 1 << 30, key_order)
        for part in range(CHAINS):
            span = slice(part * columns // CHAINS, (part + 1) * columns // CHAINS)
            scores = dot(keys, query_ref[span, :], ((1,), (1,))) * scale
            scores = jnp.where(key_order <= query_order[:, span], scores, LOWER)
            before = high_ref[:, span]
            high = jnp.maximum(before, jnp.max(scores, axis=0, keepdims=True))
            weights = jnp.exp2(scores - high)
            fade = jnp.exp2(before - high)
            high_ref[:, span] = high
            sum_ref[:, span] = sum_ref[:, span] * fade + jnp.sum(weights, axis=0, keepdims=True)
            acc_ref[:, span] = acc_ref[:, span] * fade + dot(
                values_t, weights.astype(jnp.bfloat16), ((1,), (0,))
            )
        return carry

    lax.fori_loop(0, zh + 1, step, 0)
    total = sum_ref[...]
    safe = jnp.maximum(total, 1e-30)
    attended = (acc_ref[...] / safe).astype(jnp.bfloat16)
    stat_row = lax.broadcasted_iota(jnp.int32, (STATS, columns), 0)
    stats = jnp.zeros((STATS, columns), jnp.float32)
    left = jnp.where(total > 0.0, high_ref[...] + jnp.log2(safe), LOW)
    for k in range(3):
        piece = left.astype(jnp.bfloat16).astype(jnp.float32)
        stats = jnp.where(stat_row == k, piece, stats)
        left = left - piece
    stats = stats.astype(jnp.bfloat16)
    for to_x in range(X):
        for swap in range(ZP):
            first = (to_x * ZP + swap) * ROWS
            home = (zp + swap - 2 * zp * swap) * X + to_x
            out_ref[home, :HEAD_DIM, :] = attended[:, first : first + ROWS]
            out_ref[home, HEAD_DIM:, :] = stats[:, first : first + ROWS]


def project_kernel(parts_ref, own_ref, *refs):
    other_refs, (out_ref, other_buf, total_ref, arrived) = refs[:PIECES], refs[PIECES:]
    copies = [
        pltpu.make_async_copy(ref, other_buf.at[i], arrived.at[i])
        for i, ref in enumerate(other_refs)
    ]
    for copy in copies:
        copy.start()
    logs = []
    for t in range(GROUP):
        stats = parts_ref[t, HEAD_DIM:, :].astype(jnp.float32)
        logs.append(stats[0:1] + stats[1:2] + stats[2:3])
    high = functools.reduce(jnp.maximum, logs)
    shares = [jnp.exp2(v - high) for v in logs]
    total = functools.reduce(jnp.add, shares)
    merged = jnp.zeros((HEAD_DIM, ROWS), jnp.float32)
    for t in range(GROUP):
        part = parts_ref[t, :HEAD_DIM, :].astype(jnp.float32)
        merged += part * (shares[t] / total)
    merged = merged.T.astype(jnp.bfloat16)
    attended = jnp.concatenate(
        [merged[j * HALF : (j + 1) * HALF] for j in range(C * HEADS)], axis=1
    )
    for m in range(N_MP):
        columns = slice(m * WIDTH, (m + 1) * WIDTH)
        total_ref[m] = dot(attended[:, :WIDTH], own_ref[:, columns], ((1,), (0,)))
    for copy in copies:
        copy.wait()
    for m in range(N_MP):
        columns = slice(m * WIDTH, (m + 1) * WIDTH)
        block = total_ref[m]
        for i in range(PIECES):
            rows = slice(WIDTH + i * WIDTH // PIECES, WIDTH + (i + 1) * WIDTH // PIECES)
            block += dot(attended[:, rows], other_buf[i, :, columns], ((1,), (0,)))
        out_ref[m] = block.astype(jnp.bfloat16)


def mix_kernel(sel_ref, router_ref, hidden_ref, parts_ref, out_ref):
    halves = []
    for half in range(C):
        update = jnp.zeros((HALF, WIDTH), jnp.float32)
        for y in range(Y):
            update += parts_ref[y * C + half].astype(jnp.float32)
        halves.append(update.astype(jnp.bfloat16))
    hot = one_hot(sel_ref[...])
    spread = dot(hot.astype(jnp.bfloat16), jnp.concatenate(halves, axis=0), ((1,), (0,)))
    taken = jnp.max(hot, axis=1, keepdims=True) > 0.0
    eye = lax.broadcasted_iota(jnp.int32, (CAP, CAP), 0) == lax.broadcasted_iota(
        jnp.int32, (CAP, CAP), 1
    )
    for b in range(TOK // CAP):
        rows = slice(b * CAP, (b + 1) * CAP)
        router = jnp.sum(jnp.where(eye, router_ref[:, rows], 0.0), axis=1, keepdims=True)
        before = hidden_ref[rows, :].astype(jnp.float32)
        fresh = before + router * spread[rows]
        out_ref[rows, :] = jnp.where(taken[rows], fresh, before).astype(jnp.bfloat16)


def call(kernel, out_shape, count, scratch=(), smem_first=False, loose=0, flops=0, nbytes=0, vmem=VMEM):
    specs = [in_vmem] * (count - loose) + [in_hbm] * loose
    if smem_first:
        specs[0] = in_smem
    many = isinstance(out_shape, (tuple, list))
    return pl.pallas_call(
        kernel,
        out_shape=out_shape,
        in_specs=specs,
        out_specs=[in_vmem] * len(out_shape) if many else in_vmem,
        scratch_shapes=list(scratch),
        compiler_params=pltpu.CompilerParams(vmem_limit_bytes=vmem),
        cost_estimate=pl.CostEstimate(flops=flops, bytes_accessed=nbytes, transcendentals=0),
    )


def local(
    hidden_state,
    router_weight,
    norm_gain,
    query_weight,
    kv_weight,
    out_weight,
    sel_rows,
    dest_shard,
    dest_slot,
):
    zh, zp, x = lax.axis_index("zh"), lax.axis_index("zp"), lax.axis_index("x")
    y, core = lax.axis_index("y"), lax.axis_index("c")
    is_key = y < Y // 2
    place = jnp.stack([zh, zp, x, core]).astype(jnp.int32)
    core_at = core.astype(jnp.int32)[None]
    sel = sel_rows.reshape(1, CAP)
    swap = [(0, 1), (1, 0)]

    with jax.named_scope("pick"):
        picked = call(pick_kernel, shape((N_MP, HALF, WIDTH)), 2, vmem=WHOLE)(sel, hidden_state)
    with jax.named_scope("gather_features"):
        own_rows = lax.all_to_all(picked, MP, 0, 0, tiled=True)
        deep = WIDTH // PIECES
        out_other = [
            lax.ppermute(out_weight[i * deep : (i + 1) * deep], "c", swap) for i in range(PIECES)
        ]
        own_rows, *out_other = lax.optimization_barrier((own_rows, *out_other))
        other_rows = lax.ppermute(own_rows, "c", swap)

    with jax.named_scope("touch"):
        touched = call(touch_kernel, shape((16, HEAD_DIM)), 2, loose=1)(kv_weight, picked)
    with jax.named_scope("rotation"):
        positions = ((zh * ZP + zp) * X + x) * TOK + jnp.maximum(sel_rows, 0)
        freqs = ROPE_BASE ** (-(jnp.arange(HALF_DIM, dtype=jnp.float32) * 2.0 / HEAD_DIM))
        angles = positions.astype(jnp.float32)[:, None] * freqs[None, :]
        cosine, sine = jnp.cos(angles), jnp.sin(angles)
        cos_q = jnp.concatenate([cosine, cosine], axis=1)
        sin_q = jnp.concatenate([-sine, sine], axis=1)
        cos_kv = jnp.where(is_key, cos_q, 1.0)
        sin_kv = jnp.where(is_key, sin_q, 0.0)
        lane = jnp.arange(HEAD_DIM, dtype=jnp.int32)[None, :]
        mark = jnp.where(is_key & (sel_rows < 0)[:, None] & (lane == 0), UNUSED, 0.0)

    with jax.named_scope("keys_values"):
        normed, kv = call(
            norm_kv_kernel,
            [shape((CAP, N_MP * WIDTH)), shape((CAP, HEAD_DIM))],
            9,
            smem_first=True,
            flops=2 * CAP * 4096 * HEAD_DIM,
            nbytes=3 << 20,
        )(core_at, own_rows, other_rows, norm_gain.reshape(N_MP, WIDTH), cos_kv, sin_kv, mark, kv_weight, touched)
        to_heads = [(m, 2 * m if m < Y else 2 * (m - Y) + 1) for m in range(N_MP)]
        kv = lax.ppermute(kv, MP, to_heads)
        kv = call(lay_kernel, shape((ZH, CAP, HEAD_DIM)), 1, flops=1 << 35, nbytes=64 << 20)(kv)
    with jax.named_scope("queries"):
        mine, theirs = call(
            query_kernel,
            [shape((HEADS * HALF, HEAD_DIM)), shape((HEADS * HALF, HEAD_DIM))],
            5,
            smem_first=True,
            flops=2 * CAP * N_MP * WIDTH * WIDTH,
            nbytes=3 << 20,
        )(core_at, normed, cos_q, sin_q, query_weight)
        both = jnp.concatenate([mine, theirs], axis=0)
        swapped = lax.ppermute(both, "zp", swap)
    with jax.named_scope("spread_keys_values"):
        own = lax.all_to_all(kv, "zh", 0, 0, tiled=True)
    with jax.named_scope("share_queries"):
        half = HEADS * HALF
        away = lax.ppermute(jnp.concatenate([both[half:], swapped[half:]], axis=0), "c", swap)
        queries = jnp.concatenate([both[:half], away[:half], swapped[:half], away[half:]], axis=0)
        queries = lax.all_gather(queries, "x", axis=0, tiled=True)
        own, queries = lax.optimization_barrier((own, queries))
        other = lax.ppermute(own, "c", swap)
    with jax.named_scope("attend"):
        columns = GROUP * ROWS
        parts = call(
            attend_kernel,
            shape((GROUP, HEAD_DIM + STATS, ROWS)),
            4,
            scratch=(
                pltpu.VMEM((1, columns), jnp.float32),
                pltpu.VMEM((1, columns), jnp.float32),
                pltpu.VMEM((HEAD_DIM, columns), jnp.float32),
            ),
            smem_first=True,
            flops=4 * columns * HEAD_DIM * ZH * CAP,
            nbytes=2 << 20,
        )(place, queries, own, other)
        parts = lax.all_to_all(parts, NEAR, 0, 0, tiled=True)
    with jax.named_scope("project"):
        partial = call(
            project_kernel,
            shape((N_MP, HALF, WIDTH)),
            2 + PIECES,
            loose=PIECES,
            scratch=(
                pltpu.VMEM((PIECES, WIDTH // PIECES, N_MP * WIDTH), jnp.bfloat16),
                pltpu.VMEM((N_MP, HALF, WIDTH), jnp.float32),
                pltpu.SemaphoreType.DMA((PIECES,)),
            ),
            flops=2 * CAP * WIDTH * N_MP * WIDTH,
            nbytes=5 << 20,
        )(parts, out_weight, *out_other)
        partial = lax.all_to_all(partial, MP, 0, 0, tiled=True)
    with jax.named_scope("mix"):
        return call(mix_kernel, shape((TOK, WIDTH)), 4, nbytes=2 << 20)(
            sel, router_weight.reshape(1, TOK), hidden_state, partial
        )


def solution(mesh):
    fine = Mesh(mesh.devices.reshape(ZH, ZP, X, Y, C), AXES)
    in_specs = (
        P(SEQ, MP),
        P(SEQ),
        P(),
        P(None, MP),
        P(None, MP),
        P(MP, None),
        P(SEQ),
        P(SEQ),
        P(SEQ),
    )
    return jax.shard_map(
        local, mesh=fine, in_specs=in_specs, out_specs=P(SEQ, MP), check_vma=False
    )
```

```python
import functools
import math

import jax
import jax.numpy as jnp
from jax import lax
from jax.experimental import pallas as pl
from jax.experimental.pallas import tpu as pltpu
from jax.sharding import Mesh
from jax.sharding import PartitionSpec as P

HEAD_DIM = 128
HALF_DIM = HEAD_DIM // 2
ROPE_BASE = 500000.0
EPS = 1e-05

ZH, ZP, X, Y, C = 8, 2, 4, 8, 2
AXES = ("zh", "zp", "x", "y", "c")
SEQ, MP = ("zh", "zp", "x"), ("y", "c")
NEAR = ("zp", "x")
GROUP = ZP * X
N_MP = Y * C
CAP = 128
HALF = CAP // C
TOK = 512
WIDTH = 256
HEADS = WIDTH // HEAD_DIM
ROWS = C * HEADS * HALF
STATS = 16
UNUSED = 1e30
STRIPS = 4
PIECES = 4
CHAINS = 1
LOW, LOWER = -1e30, -2e30
VMEM = 48 * 1024 * 1024
WHOLE = 62 * 1024 * 1024

in_vmem = pl.BlockSpec(memory_space=pltpu.VMEM)
in_smem = pl.BlockSpec(memory_space=pltpu.SMEM)
in_hbm = pl.BlockSpec(memory_space=pltpu.HBM)


def shape(dims, dtype=jnp.bfloat16):
    return jax.ShapeDtypeStruct(dims, dtype)


def dot(a, b, contract):
    return lax.dot_general(a, b, (contract, ((), ())), preferred_element_type=jnp.float32)


def one_hot(sel_row):
    rows = lax.broadcasted_iota(jnp.int32, (TOK, CAP), 0)
    return jnp.where(rows == sel_row, 1.0, 0.0)


def turn(head, cosine, sine):
    return head * cosine + pltpu.roll(head, HALF_DIM, 1) * sine


def pick_kernel(sel_ref, hidden_ref, out_ref):
    hot = one_hot(sel_ref[...]).astype(jnp.bfloat16)
    picked = dot(hot, hidden_ref[...], ((0,), (0,))).astype(jnp.bfloat16)
    for m in range(N_MP):
        half = m % C
        out_ref[m] = picked[half * HALF : (half + 1) * HALF]


def touch_kernel(weight_ref, after_ref, out_ref):
    del after_ref
    out_ref[...] = weight_ref[:16, :HEAD_DIM]


def norm_kv_kernel(
    core_ref,
    own_ref,
    other_ref,
    gain_ref,
    cos_ref,
    sin_ref,
    mark_ref,
    weight_ref,
    after_ref,
    normed_ref,
    kv_ref,
):
    del after_ref
    core = core_ref[0]
    for ref, half in ((own_ref, core), (other_ref, 1 - core)):
        square = jnp.zeros((HALF, WIDTH), jnp.float32)
        for m in range(N_MP):
            vals = ref[m].astype(jnp.float32)
            square += vals * vals
        mean = jnp.sum(square, axis=1, keepdims=True) / (N_MP * WIDTH)
        inverse = lax.rsqrt(mean + EPS)
        first = pl.multiple_of(half * HALF, HALF)
        for m in range(N_MP):
            vals = ref[m].astype(jnp.float32) * inverse * gain_ref[m : m + 1, :]
            normed_ref[pl.ds(first, HALF), m * WIDTH : (m + 1) * WIDTH] = vals.astype(jnp.bfloat16)
    total = dot(normed_ref[...], weight_ref[...], ((1,), (0,)))
    kv_ref[...] = (turn(total, cos_ref[...], sin_ref[...]) + mark_ref[...]).astype(jnp.bfloat16)


def lay_kernel(kv_ref, out_ref):
    for t in range(ZH):
        out_ref[t] = kv_ref[...]


def query_kernel(core_ref, normed_ref, cos_ref, sin_ref, weight_ref, mine_ref, theirs_ref):
    core = core_ref[0]
    total = dot(normed_ref[...], weight_ref[...], ((1,), (0,)))
    for h in range(HEADS):
        head = total[:, h * HEAD_DIM : (h + 1) * HEAD_DIM]
        turned = turn(head, cos_ref[...], sin_ref[...]).astype(jnp.bfloat16)
        lower, upper = turned[:HALF], turned[HALF:]
        rows = slice(h * HALF, (h + 1) * HALF)
        mine_ref[rows, :] = jnp.where(core == 0, lower, upper)
        theirs_ref[rows, :] = jnp.where(core == 0, upper, lower)


def attend_kernel(place_ref, query_ref, own_ref, other_ref, out_ref, high_ref, sum_ref, acc_ref):
    zh, zp, x, c = place_ref[0], place_ref[1], place_ref[2], place_ref[3]
    columns = GROUP * ROWS
    scale = math.log2(math.e) / math.sqrt(HEAD_DIM)
    high_ref[...] = jnp.full(high_ref.shape, LOW, jnp.float32)
    sum_ref[...] = jnp.zeros(sum_ref.shape, jnp.float32)
    acc_ref[...] = jnp.zeros(acc_ref.shape, jnp.float32)
    column = lax.broadcasted_iota(jnp.int32, (1, columns), 1)
    swapped = column // ROWS % ZP
    query_zp = zp + swapped - 2 * zp * swapped
    query_shard = (zh * ZP + query_zp) * X + column // (ZP * ROWS)
    query_order = query_shard * CAP + c * HALF + column % HALF

    def step(far, carry):
        own, other = own_ref[far], other_ref[far]
        keys = jnp.where(c == 0, own, other)
        values_t = jnp.where(c == 0, other, own).T
        entry = lax.broadcasted_iota(jnp.int32, (CAP, 1), 0)
        key_order = ((far * ZP + zp) * X + x) * CAP + entry
        unused = keys[:, 0:1].astype(jnp.float32) > 0.1 * UNUSED
        key_order = jnp.where(unused, 1 << 30, key_order)
        for part in range(CHAINS):
            span = slice(part * columns // CHAINS, (part + 1) * columns // CHAINS)
            scores = dot(keys, query_ref[span, :], ((1,), (1,))) * scale
            scores = jnp.where(key_order <= query_order[:, span], scores, LOWER)
            before = high_ref[:, span]
            high = jnp.maximum(before, jnp.max(scores, axis=0, keepdims=True))
            weights = jnp.exp2(scores - high)
            fade = jnp.exp2(before - high)
            high_ref[:, span] = high
            sum_ref[:, span] = sum_ref[:, span] * fade + jnp.sum(weights, axis=0, keepdims=True)
            acc_ref[:, span] = acc_ref[:, span] * fade + dot(
                values_t, weights.astype(jnp.bfloat16), ((1,), (0,))
            )
        return carry

    lax.fori_loop(0, zh + 1, step, 0)
    total = sum_ref[...]
    safe = jnp.maximum(total, 1e-30)
    attended = (acc_ref[...] / safe).astype(jnp.bfloat16)
    stat_row = lax.broadcasted_iota(jnp.int32, (STATS, columns), 0)
    stats = jnp.zeros((STATS, columns), jnp.float32)
    left = jnp.where(total > 0.0, high_ref[...] + jnp.log2(safe), LOW)
    for k in range(3):
        piece = left.astype(jnp.bfloat16).astype(jnp.float32)
        stats = jnp.where(stat_row == k, piece, stats)
        left = left - piece
    stats = stats.astype(jnp.bfloat16)
    for to_x in range(X):
        for swap in range(ZP):
            first = (to_x * ZP + swap) * ROWS
            home = (zp + swap - 2 * zp * swap) * X + to_x
            out_ref[home, :HEAD_DIM, :] = attended[:, first : first + ROWS]
            out_ref[home, HEAD_DIM:, :] = stats[:, first : first + ROWS]


def project_kernel(parts_ref, own_ref, *refs):
    other_refs, (out_ref, other_buf, total_ref, arrived) = refs[:PIECES], refs[PIECES:]
    strip = N_MP // STRIPS * WIDTH
    copies = []
    for k in range(STRIPS):
        span = pl.ds(k * strip, strip)
        for i, ref in enumerate(other_refs):
            copies.append(
                pltpu.make_async_copy(
                    ref.at[:, span], other_buf.at[i, :, span], arrived.at[k * PIECES + i]
                )
            )
    for copy in copies:
        copy.start()
    logs = []
    for t in range(GROUP):
        stats = parts_ref[t, HEAD_DIM:, :].astype(jnp.float32)
        logs.append(stats[0:1] + stats[1:2] + stats[2:3])
    high = functools.reduce(jnp.maximum, logs)
    shares = [jnp.exp2(v - high) for v in logs]
    total = functools.reduce(jnp.add, shares)
    merged = jnp.zeros((HEAD_DIM, ROWS), jnp.float32)
    for t in range(GROUP):
        part = parts_ref[t, :HEAD_DIM, :].astype(jnp.float32)
        merged += part * (shares[t] / total)
    merged = merged.T.astype(jnp.bfloat16)
    attended = jnp.concatenate(
        [merged[j * HALF : (j + 1) * HALF] for j in range(C * HEADS)], axis=1
    )
    for m in range(N_MP):
        columns = slice(m * WIDTH, (m + 1) * WIDTH)
        total_ref[m] = dot(attended[:, :WIDTH], own_ref[:, columns], ((1,), (0,)))
    for m in range(N_MP):
        if m % (N_MP // STRIPS) == 0:
            first = m // (N_MP // STRIPS) * PIECES
            for copy in copies[first : first + PIECES]:
                copy.wait()
        columns = slice(m * WIDTH, (m + 1) * WIDTH)
        block = total_ref[m]
        for i in range(PIECES):
            rows = slice(WIDTH + i * WIDTH // PIECES, WIDTH + (i + 1) * WIDTH // PIECES)
            block += dot(attended[:, rows], other_buf[i, :, columns], ((1,), (0,)))
        out_ref[m] = block.astype(jnp.bfloat16)


def mix_kernel(sel_ref, router_ref, hidden_ref, parts_ref, out_ref):
    halves = []
    for half in range(C):
        update = jnp.zeros((HALF, WIDTH), jnp.float32)
        for y in range(Y):
            update += parts_ref[y * C + half].astype(jnp.float32)
        halves.append(update.astype(jnp.bfloat16))
    hot = one_hot(sel_ref[...])
    spread = dot(hot.astype(jnp.bfloat16), jnp.concatenate(halves, axis=0), ((1,), (0,)))
    taken = jnp.max(hot, axis=1, keepdims=True) > 0.0
    eye = lax.broadcasted_iota(jnp.int32, (CAP, CAP), 0) == lax.broadcasted_iota(
        jnp.int32, (CAP, CAP), 1
    )
    for b in range(TOK // CAP):
        rows = slice(b * CAP, (b + 1) * CAP)
        router = jnp.sum(jnp.where(eye, router_ref[:, rows], 0.0), axis=1, keepdims=True)
        before = hidden_ref[rows, :].astype(jnp.float32)
        fresh = before + router * spread[rows]
        out_ref[rows, :] = jnp.where(taken[rows], fresh, before).astype(jnp.bfloat16)


def call(kernel, out_shape, count, scratch=(), smem_first=False, loose=0, flops=0, nbytes=0, vmem=VMEM):
    specs = [in_vmem] * (count - loose) + [in_hbm] * loose
    if smem_first:
        specs[0] = in_smem
    many = isinstance(out_shape, (tuple, list))
    return pl.pallas_call(
        kernel,
        out_shape=out_shape,
        in_specs=specs,
        out_specs=[in_vmem] * len(out_shape) if many else in_vmem,
        scratch_shapes=list(scratch),
        compiler_params=pltpu.CompilerParams(vmem_limit_bytes=vmem),
        cost_estimate=pl.CostEstimate(flops=flops, bytes_accessed=nbytes, transcendentals=0),
    )


def local(
    hidden_state,
    router_weight,
    norm_gain,
    query_weight,
    kv_weight,
    out_weight,
    sel_rows,
    dest_shard,
    dest_slot,
):
    zh, zp, x = lax.axis_index("zh"), lax.axis_index("zp"), lax.axis_index("x")
    y, core = lax.axis_index("y"), lax.axis_index("c")
    is_key = y < Y // 2
    place = jnp.stack([zh, zp, x, core]).astype(jnp.int32)
    core_at = core.astype(jnp.int32)[None]
    sel = sel_rows.reshape(1, CAP)
    swap = [(0, 1), (1, 0)]

    with jax.named_scope("pick"):
        picked = call(pick_kernel, shape((N_MP, HALF, WIDTH)), 2, vmem=WHOLE)(sel, hidden_state)
    with jax.named_scope("gather_features"):
        own_rows = lax.all_to_all(picked, MP, 0, 0, tiled=True)
        deep = WIDTH // PIECES
        out_other = [
            lax.ppermute(out_weight[i * deep : (i + 1) * deep], "c", swap) for i in range(PIECES)
        ]
        own_rows, *out_other = lax.optimization_barrier((own_rows, *out_other))
        other_rows = lax.ppermute(own_rows, "c", swap)

    with jax.named_scope("touch"):
        touched = call(touch_kernel, shape((16, HEAD_DIM)), 2, loose=1)(kv_weight, picked)
    with jax.named_scope("rotation"):
        positions = ((zh * ZP + zp) * X + x) * TOK + jnp.maximum(sel_rows, 0)
        freqs = ROPE_BASE ** (-(jnp.arange(HALF_DIM, dtype=jnp.float32) * 2.0 / HEAD_DIM))
        angles = positions.astype(jnp.float32)[:, None] * freqs[None, :]
        cosine, sine = jnp.cos(angles), jnp.sin(angles)
        cos_q = jnp.concatenate([cosine, cosine], axis=1)
        sin_q = jnp.concatenate([-sine, sine], axis=1)
        cos_kv = jnp.where(is_key, cos_q, 1.0)
        sin_kv = jnp.where(is_key, sin_q, 0.0)
        lane = jnp.arange(HEAD_DIM, dtype=jnp.int32)[None, :]
        mark = jnp.where(is_key & (sel_rows < 0)[:, None] & (lane == 0), UNUSED, 0.0)

    with jax.named_scope("keys_values"):
        normed, kv = call(
            norm_kv_kernel,
            [shape((CAP, N_MP * WIDTH)), shape((CAP, HEAD_DIM))],
            9,
            smem_first=True,
            flops=2 * CAP * 4096 * HEAD_DIM,
            nbytes=3 << 20,
        )(core_at, own_rows, other_rows, norm_gain.reshape(N_MP, WIDTH), cos_kv, sin_kv, mark, kv_weight, touched)
        to_heads = [(m, 2 * m if m < Y else 2 * (m - Y) + 1) for m in range(N_MP)]
        kv = lax.ppermute(kv, MP, to_heads)
        kv = call(lay_kernel, shape((ZH, CAP, HEAD_DIM)), 1, flops=1 << 35, nbytes=64 << 20)(kv)
    with jax.named_scope("queries"):
        mine, theirs = call(
            query_kernel,
            [shape((HEADS * HALF, HEAD_DIM)), shape((HEADS * HALF, HEAD_DIM))],
            5,
            smem_first=True,
            flops=2 * CAP * N_MP * WIDTH * WIDTH,
            nbytes=3 << 20,
        )(core_at, normed, cos_q, sin_q, query_weight)
        both = jnp.concatenate([mine, theirs], axis=0)
        swapped = lax.ppermute(both, "zp", swap)
    with jax.named_scope("spread_keys_values"):
        own = lax.all_to_all(kv, "zh", 0, 0, tiled=True)
    with jax.named_scope("share_queries"):
        half = HEADS * HALF
        away = lax.ppermute(jnp.concatenate([both[half:], swapped[half:]], axis=0), "c", swap)
        queries = jnp.concatenate([both[:half], away[:half], swapped[:half], away[half:]], axis=0)
        queries = lax.all_gather(queries, "x", axis=0, tiled=True)
        own, queries = lax.optimization_barrier((own, queries))
        other = lax.ppermute(own, "c", swap)
    with jax.named_scope("attend"):
        columns = GROUP * ROWS
        parts = call(
            attend_kernel,
            shape((GROUP, HEAD_DIM + STATS, ROWS)),
            4,
            scratch=(
                pltpu.VMEM((1, columns), jnp.float32),
                pltpu.VMEM((1, columns), jnp.float32),
                pltpu.VMEM((HEAD_DIM, columns), jnp.float32),
            ),
            smem_first=True,
            flops=4 * columns * HEAD_DIM * ZH * CAP,
            nbytes=2 << 20,
        )(place, queries, own, other)
        parts = lax.all_to_all(parts, NEAR, 0, 0, tiled=True)
    with jax.named_scope("project"):
        partial = call(
            project_kernel,
            shape((N_MP, HALF, WIDTH)),
            2 + PIECES,
            loose=PIECES,
            scratch=(
                pltpu.VMEM((PIECES, WIDTH // PIECES, N_MP * WIDTH), jnp.bfloat16),
                pltpu.VMEM((N_MP, HALF, WIDTH), jnp.float32),
                pltpu.SemaphoreType.DMA((STRIPS * PIECES,)),
            ),
            flops=2 * CAP * WIDTH * N_MP * WIDTH,
            nbytes=5 << 20,
        )(parts, out_weight, *out_other)
        partial = lax.all_to_all(partial, MP, 0, 0, tiled=True)
    with jax.named_scope("mix"):
        return call(mix_kernel, shape((TOK, WIDTH)), 4, nbytes=2 << 20)(
            sel, router_weight.reshape(1, TOK), hidden_state, partial
        )


def solution(mesh):
    fine = Mesh(mesh.devices.reshape(ZH, ZP, X, Y, C), AXES)
    in_specs = (
        P(SEQ, MP),
        P(SEQ),
        P(),
        P(None, MP),
        P(None, MP),
        P(MP, None),
        P(SEQ),
        P(SEQ),
        P(SEQ),
    )
    return jax.shard_map(
        local, mesh=fine, in_specs=in_specs, out_specs=P(SEQ, MP), check_vma=False
    )
```
